32 devices in a mesh: batch: 2 (over x), ctx: 4 (over z), tp: 4 (over y, core).
Axes of the slice: x: 2, y: 2, z: 4, core: 2. Of those that a mesh axis runs over, the one named last changes fastest.
Arguments:
- frames: bfloat16 [1536, 1536], P(('batch', 'ctx'), 'tp'), parts along dimension 0, may hold values from -6 to 6
- attn_gain: float32 [1536], replicated, may hold values from 0.5 to 1.5
- query_key_value: bfloat16 [3, 1536, 1536], P(None, None, 'tp'), may hold values from -1 to 1
- out_weight: bfloat16 [1536, 1536], P('tp'), may hold values from -6 to 6
- conv_gain: float32 [1536], replicated, may hold values from 0.5 to 1.5
- glu_weight: bfloat16 [2, 1536, 1536], P(None, None, 'tp'), may hold values from -0.15625 to 0.15625
- depth_kernel: bfloat16 [31, 1536], P(None, 'tp'), may hold values from -1 to 1
- depth_bias: float32 [1536], P('tp'), may hold values from -4 to 4
- proj_weight: bfloat16 [1536, 1536], P('tp'), may hold values from -0.15625 to 0.15625
Outputs:
- layer_out: bfloat16 [1536, 1536], P(('batch', 'ctx'), 'tp'), parts along dimension 0
The draws below stay inside these ranges and needn't reach their ends.
There are 2 independent parts, one for each index of `batch`. The reference program is written for one: setup_inputs(seed, part) draws one part's arguments, and reference() takes and returns one part's arrays. A program takes and returns all parts, laid end to end along the dimension named above; an argument that names none is the same for every part. Nothing has to cross between parts.
All inputs are finite; a program needn't handle non-finite values.
Results may differ from the reference program's by a relative error of at most 0.019.
Values may be sent and summed in bfloat16 or wider, within the bound.
A program may use at most 128 MiB of HBM per device.

```python
import math
import jax
import jax.numpy as jnp
from jax import lax

D = 1536
HEADS = 16
HEAD = 96
KERNEL = 31
FRAMES = 768


def draw_query_key_value(key, part):
    key = jax.random.fold_in(key, 11)
    first_key = jax.random.fold_in(key, 0)
    base = jax.random.normal(first_key, (3, D, D), jnp.float32) / math.sqrt(D)
    return jnp.clip(base, -1.0, 1.0).astype(jnp.bfloat16)


def shard_levels(key, shape, cuts, least, high):
    loudness = 1.0
    for position, blocks in cuts:
        heights = jax.random.uniform(jax.random.fold_in(jax.random.fold_in(key, 6), position), (blocks,), jnp.float32, least / len(cuts), high / len(cuts))
        loudness = loudness * jnp.repeat(jnp.exp(heights), shape[position] // blocks).reshape((-1,) + (1,) * (len(shape) - 1 - position))
    return loudness


def noise(key, shape, deviation, most, shards=(), kind=jnp.bfloat16):
    level = shard_levels(key, shape, shards, -0.22, 0.18) if shards else 1.0
    entries = jax.random.normal(key, shape, jnp.float32) * deviation * level
    return jnp.minimum(jnp.maximum(entries, -most), most).astype(kind)


def setup_inputs(seed: int = 0, part: int = 0) -> dict:
    seeds = jax.random.split(jax.random.key(seed), 10)
    part_splits = jax.random.split(jax.random.fold_in(seeds[9], part), 10)
    return {
        "frames": noise(part_splits[0], (FRAMES, D), 1.0, 6.0, ((0, 4), (1, 4))),
        "attn_gain": jnp.clip(jax.random.uniform(seeds[1], (D,), jnp.float32, 0.5, 1.5), 0.5, 1.5),
        "query_key_value": draw_query_key_value(jax.random.fold_in(seeds[9], 71), part),
        "out_weight": noise(seeds[3], (D, D), 1.0, 6.0, ((0, 4),)),
        "conv_gain": jnp.clip(jax.random.uniform(seeds[4], (D,), jnp.float32, 0.5, 1.5), 0.5, 1.5),
        "glu_weight": noise(seeds[5], (2, D, D), D ** -0.5, 0.15625, ((2, 4),)),
        "depth_kernel": noise(seeds[6], (KERNEL, D), KERNEL ** -0.5, 1.0, ((1, 4),)),
        "depth_bias": noise(seeds[7], (D,), 1.0, 4.0, ((0, 4),), jnp.float32),
        "proj_weight": noise(seeds[8], (D, D), D ** -0.5, 0.15625, ((0, 4),)),
    }


def layer_norm(inputs, gain):
    inputs = inputs.astype(jnp.float32)
    average = lax.optimization_barrier(jnp.mean(inputs, axis=-1, keepdims=True))
    centered = inputs - average
    variance = lax.optimization_barrier(jnp.mean(centered * centered, axis=-1, keepdims=True))
    return (centered * lax.rsqrt(variance + 1e-05) * gain.astype(jnp.float32)).astype(jnp.bfloat16)

def reference(frames, attn_gain, query_key_value, out_weight, conv_gain, glu_weight, depth_kernel, depth_bias, proj_weight):
    normed = layer_norm(frames, attn_gain)
    queries = jnp.dot(normed, query_key_value[0], preferred_element_type=jnp.float32).astype(jnp.bfloat16)
    key_rows = jnp.dot(normed, query_key_value[1], preferred_element_type=jnp.float32).astype(jnp.bfloat16)
    value_rows = jnp.dot(normed, query_key_value[2], preferred_element_type=jnp.float32).astype(jnp.bfloat16)
    query_heads = queries.reshape(FRAMES, HEADS, HEAD).astype(jnp.float32)
    key_heads = key_rows.reshape(FRAMES, HEADS, HEAD).astype(jnp.float32)
    value_heads = value_rows.reshape(FRAMES, HEADS, HEAD).astype(jnp.float32)
    score_scale = 1.0 / math.sqrt(HEAD)
    block_len = math.gcd(FRAMES, 256)

    def attend(start):
        query_block = lax.dynamic_slice_in_dim(query_heads, start, block_len, 0)
        scores = jnp.einsum('qhd,khd->hqk', query_block, key_heads) * score_scale
        row_max = lax.optimization_barrier(jnp.max(scores, axis=-1, keepdims=True))
        weights = jnp.exp(scores - row_max)
        denominator = lax.optimization_barrier(jnp.sum(weights, axis=-1))
        rounded = weights.astype(jnp.bfloat16).astype(jnp.float32)
        summed = jnp.einsum('hqk,khd->qhd', rounded, value_heads)
        return (summed / jnp.transpose(denominator)[:, :, None]).astype(jnp.bfloat16)
    starts = jnp.arange(FRAMES // block_len, dtype=jnp.int32) * block_len
    context = lax.map(attend, starts).reshape(FRAMES, D)
    attended = jnp.dot(context, out_weight, preferred_element_type=jnp.float32)
    middle = (frames.astype(jnp.float32) + attended).astype(jnp.bfloat16)
    normed_conv = layer_norm(middle, conv_gain)
    value_half = jnp.dot(normed_conv, glu_weight[0], preferred_element_type=jnp.float32)
    gate_half = jnp.dot(normed_conv, glu_weight[1], preferred_element_type=jnp.float32)
    glu = (value_half * jax.nn.sigmoid(gate_half)).astype(jnp.bfloat16)
    reach = KERNEL // 2
    padded = jnp.pad(glu.astype(jnp.float32), ((reach, reach), (0, 0)))
    convolved = jnp.zeros((FRAMES, D), jnp.float32)
    for kernel_tap in range(KERNEL):
        convolved = convolved + padded[kernel_tap:kernel_tap + FRAMES] * depth_kernel[kernel_tap].astype(jnp.float32)
    activated = jax.nn.silu(convolved + depth_bias.astype(jnp.float32)).astype(jnp.bfloat16)
    projected = jnp.dot(activated, proj_weight, preferred_element_type=jnp.float32)
    return (middle.astype(jnp.float32) + projected).astype(jnp.bfloat16)
```

```python
import functools
import math

import jax
import jax.numpy as jnp
from jax import lax
from jax.experimental import pallas as pl
from jax.experimental.pallas import tpu as pltpu
from jax.sharding import PartitionSpec as P

HEAD = 96
HALO = 16
ROW_CHUNKS = 2
WINDOW = 256
MESH = pl.DeviceIdType.MESH


def layer_norm(inputs, gain):
    inputs = inputs.astype(jnp.float32)
    average = jnp.mean(inputs, axis=-1, keepdims=True)
    centered = inputs - average
    variance = jnp.mean(centered * centered, axis=-1, keepdims=True)
    return (centered * lax.rsqrt(variance + 1e-05) * gain).astype(jnp.bfloat16)


def depthwise(padded, kernel, bias, count):
    convolved = jnp.zeros((count, padded.shape[1]), jnp.float32)
    for kernel_tap in range(kernel.shape[0]):
        convolved = convolved + padded[kernel_tap : kernel_tap + count].astype(
            jnp.float32
        ) * kernel[kernel_tap].astype(jnp.float32)
    return jax.nn.silu(convolved + bias).astype(jnp.bfloat16)


def per_device(
    frames,
    attn_gain,
    query_key_value,
    out_weight,
    conv_gain,
    glu_weight,
    depth_kernel,
    depth_bias,
    proj_weight,
):
    frame_rows = frames.shape[0]
    local_cols = frames.shape[1]
    heads_here = query_key_value.shape[2] // HEAD
    whole_rows = lax.all_gather(frames, "tp", axis=1, tiled=True)
    normed = layer_norm(whole_rows, attn_gain)
    projected = jnp.einsum(
        "td,gdc->gtc", normed, query_key_value, preferred_element_type=jnp.float32
    ).astype(jnp.bfloat16)
    score_scale = 1.0 / math.sqrt(HEAD)
    query_heads = projected[0].reshape(frame_rows, heads_here, HEAD)
    initial = (
        jnp.full((heads_here, frame_rows), -1e30, jnp.float32),
        jnp.zeros((heads_here, frame_rows), jnp.float32),
        jnp.zeros((frame_rows, heads_here, HEAD), jnp.float32),
    )
    pieces = (
        lax.all_gather(projected[1], "ctx", axis=0, tiled=True),
        lax.all_gather(projected[2], "ctx", axis=0, tiled=True),
    )
    key_count = pieces[0].shape[0]
    block_len = 1024 if key_count > 1024 and key_count % 1024 == 0 else key_count
    key_blocks = pieces[0].reshape(key_count // block_len, block_len, heads_here, HEAD)
    value_blocks = pieces[1].reshape(key_count // block_len, block_len, heads_here, HEAD)

    def one_block(running, pieces_now):
        running_max, denominator, weighted = running
        key_block, value_block = pieces_now
        scores = (
            jnp.einsum("qhd,khd->hqk", query_heads, key_block, preferred_element_type=jnp.float32)
            * score_scale
        )
        new_max = jnp.maximum(running_max, jnp.max(scores, axis=-1))
        weights = jnp.exp(scores - new_max[:, :, None])
        rescale = jnp.exp(running_max - new_max)
        denominator = denominator * rescale + jnp.sum(weights, axis=-1)
        added = jnp.einsum(
            "hqk,khd->qhd",
            weights.astype(jnp.bfloat16),
            value_block,
            preferred_element_type=jnp.float32,
        )
        weighted = weighted * jnp.transpose(rescale)[:, :, None] + added
        return ((new_max, denominator, weighted), None)

    result, _ = lax.scan(one_block, initial, (key_blocks, value_blocks))
    running_max, denominator, weighted = result
    context = (
        (weighted / jnp.transpose(denominator)[:, :, None])
        .reshape(frame_rows, local_cols)
        .astype(jnp.bfloat16)
    )
    attn_terms = jnp.dot(context, out_weight, preferred_element_type=jnp.float32)
    summed = lax.psum(attn_terms.astype(jnp.bfloat16), "tp").astype(jnp.float32)
    middle_whole = (whole_rows.astype(jnp.float32) + summed).astype(jnp.bfloat16)
    middle = lax.dynamic_slice_in_dim(
        middle_whole, lax.axis_index("tp") * local_cols, local_cols, 1
    )
    normed_conv = layer_norm(middle_whole, conv_gain)
    halves = jnp.einsum("td,gdc->gtc", normed_conv, glu_weight, preferred_element_type=jnp.float32)
    glu = (halves[0] * jax.nn.sigmoid(halves[1])).astype(jnp.bfloat16)
    reach = depth_kernel.shape[0] // 2
    regrouped = lax.all_to_all(glu, "ctx", split_axis=1, concat_axis=0, tiled=True)
    group_cols = regrouped.shape[1]
    offset_cols = lax.axis_index("ctx") * group_cols
    kernel_part = lax.dynamic_slice_in_dim(depth_kernel, offset_cols, group_cols, 1)
    bias_part = lax.dynamic_slice_in_dim(depth_bias, offset_cols, group_cols, 0)
    padded = jnp.pad(regrouped, ((reach, reach), (0, 0)))
    activated_part = depthwise(padded, kernel_part, bias_part, regrouped.shape[0])
    activated = lax.all_to_all(activated_part, "ctx", split_axis=0, concat_axis=1, tiled=True)
    conv_terms = jnp.dot(activated, proj_weight, preferred_element_type=jnp.float32)
    conv_sum = lax.psum_scatter(
        conv_terms.astype(jnp.bfloat16), "tp", scatter_dimension=1, tiled=True
    ).astype(jnp.float32)
    return (middle.astype(jnp.float32) + conv_sum).astype(jnp.bfloat16)


def pick(table, row, column):
    value = 0
    for index, line in enumerate(table):
        value = value + jnp.where(row == index, line[column], 0)
    return value


def norm_rows(parts, gain, store):
    width = sum(part.shape[-1] for part in parts)
    total = sum(jnp.sum(part, axis=-1, keepdims=True) for part in parts)
    average = total / width
    centered = [part - average for part in parts]
    squares = sum(jnp.sum(part * part, axis=-1, keepdims=True) for part in centered)
    scale = lax.rsqrt(squares / width + 1e-05)
    start = 0
    for index, part in enumerate(centered):
        stop = start + part.shape[-1]
        store(index, (part * scale * gain[:, start:stop]).astype(jnp.bfloat16))
        start = stop


def fused_kernel(
    ctx_size,
    tp_size,
    frames,
    attn_gain,
    qkv,
    out_w,
    conv_gain,
    glu_w,
    depth_k,
    depth_b,
    proj_w,
    out,
    w_qkv,
    w_out,
    w_glu,
    w_proj,
    taps,
    taps32,
    gathered,
    normed,
    q_all,
    k_all,
    v_all,
    context_out,
    context_in,
    part32,
    part16,
    pair_in,
    pair_sum,
    peer_in,
    middle,
    glu16,
    halo_low,
    halo_high,
    padded,
    act,
    conv32,
    conv16,
    conv_pair_in,
    conv_keep,
    conv_send,
    conv_peer_in,
    local_sem,
    gather_recv,
    sib_send,
    peer_send,
    up_send,
    down_send,
    ctx_send,
    ctx_recv,
    stage_send,
    stage_recv,
    halo_send,
    halo_recv,
):
    c = lax.axis_index("ctx")
    t = lax.axis_index("tp")
    y = t // 2
    k = t % 2
    sibling = y * 2 + (1 - k)
    peer = (1 - y) * 2 + k
    diagonal = (1 - y) * 2 + (1 - k)
    rows, cols = frames.shape
    step_rows = rows // ROW_CHUNKS

    def remote(source, target, send, receive, **device):
        return pltpu.make_async_remote_copy(
            src_ref=source,
            dst_ref=target,
            send_sem=send,
            recv_sem=receive,
            device_id=device,
            device_id_type=MESH,
        )

    first_col = c * HEAD
    window = jnp.minimum(first_col // 128, (cols - WINDOW) // 128)
    shift = first_col - window * 128
    window_cols = pl.ds(pl.multiple_of(window * 128, 128), WINDOW)

    def block(ctx_index, tp_index):
        return gathered.at[tp_index, pl.ds(pl.multiple_of(ctx_index * rows, 16), rows)]

    local = [pltpu.make_async_copy(frames, block(c, t), local_sem.at[0])]
    for i in range(3):
        local.append(
            pltpu.make_async_copy(
                qkv.at[i, :, window_cols],
                w_qkv.at[:, pl.ds(i * WINDOW, WINDOW)],
                local_sem.at[1 + i],
            )
        )
    local.append(pltpu.make_async_copy(out_w, w_out, local_sem.at[4]))
    for i in range(2):
        local.append(
            pltpu.make_async_copy(
                glu_w.at[i], w_glu.at[:, pl.ds(i * cols, cols)], local_sem.at[5 + i]
            )
        )
    local.append(pltpu.make_async_copy(proj_w, w_proj, local_sem.at[7]))
    local.append(pltpu.make_async_copy(depth_k, taps, local_sem.at[8]))

    barrier = pltpu.get_barrier_semaphore()
    for other in (sibling, peer):
        pl.semaphore_signal(barrier, inc=1, device_id={"tp": other}, device_id_type=MESH)
    for hop in range(1, ctx_size):
        pl.semaphore_signal(
            barrier, inc=1, device_id={"ctx": (c + hop) % ctx_size}, device_id_type=MESH
        )
    for copy in local:
        copy.start()
    pl.semaphore_wait(barrier, 2 + ctx_size - 1)

    def to_peer(index, source):
        return remote(source, block(index, t), peer_send.at[index], gather_recv.at[index, t], tp=peer)

    def to_sibling(index, half, source):
        owner = half * 2 + k
        return remote(
            source,
            block(index, owner),
            sib_send.at[index, half],
            gather_recv.at[index, owner],
            tp=sibling,
        )

    def up(index, source):
        return remote(
            source, block(index, t), up_send.at[index], gather_recv.at[index, t], ctx=c + 1
        )

    def down(index, source):
        return remote(
            source, block(index, t), down_send.at[index], gather_recv.at[index, t], ctx=c - 1
        )

    def arrived(index, owner):
        here = block(index, owner)
        remote(here, here, peer_send.at[index], gather_recv.at[index, owner], tp=peer).wait_recv()

    has_up = c + 1 < ctx_size
    has_down = c > 0

    pl.when(has_up)(lambda: up(c, frames).start())
    pl.when(has_down)(lambda: down(c, frames).start())
    to_peer(c, frames).start()
    to_sibling(c, y, frames).start()

    order = []
    for place in range(ctx_size):
        line = [place]
        for hop in range(1, ctx_size):
            line += [i for i in (place - hop, place + hop) if 0 <= i < ctx_size]
        order.append(line)

    key_lane = lax.broadcasted_iota(jnp.int32, (rows, WINDOW), 1)
    in_head = (key_lane >= shift) & (key_lane < shift + HEAD)
    select_row = lax.broadcasted_iota(jnp.int32, (WINDOW, 128), 0)
    select_col = lax.broadcasted_iota(jnp.int32, (WINDOW, 128), 1)
    select = ((select_row == select_col + shift) & (select_col < HEAD)).astype(jnp.bfloat16)

    def project(place):
        index = pick(order, c, place)
        arrived(index, sibling)
        arrived(index, diagonal)
        start = pl.multiple_of(index * rows, 16)
        sub = rows // 4

        def norm_step(step, carry):
            at = pl.ds(pl.multiple_of(start + step * sub, 16), sub)
            to = pl.ds(pl.multiple_of(step * sub, 16), sub)

            def store(part, value):
                normed[to, part * cols : (part + 1) * cols] = value

            norm_rows(
                [gathered[i, at, :].astype(jnp.float32) for i in range(tp_size)],
                attn_gain[...],
                store,
            )
            return carry

        lax.fori_loop(0, 4, norm_step, 0)
        here = pl.ds(start, rows)
        projected = jnp.dot(normed[...], w_qkv[...], preferred_element_type=jnp.float32)
        q_all[here, :] = jnp.where(in_head, projected[:, :WINDOW], 0.0).astype(jnp.bfloat16)
        k_all[here, :] = projected[:, WINDOW : 2 * WINDOW].astype(jnp.bfloat16)
        v_all[here, :] = jnp.dot(
            projected[:, 2 * WINDOW :].astype(jnp.bfloat16),
            select,
            preferred_element_type=jnp.float32,
        ).astype(jnp.bfloat16)

    arrived(c, peer)
    to_sibling(c, 1 - y, block(c, peer)).start()
    for hop in range(1, ctx_size):

        @pl.when(c >= hop)
        def _():
            index = c - hop
            arrived(index, t)
            source = block(index, t)
            pl.when(has_up)(lambda: up(index, source).start())
            to_peer(index, source).start()
            to_sibling(index, y, source).start()

        @pl.when(c + hop < ctx_size)
        def _():
            index = c + hop
            arrived(index, t)
            source = block(index, t)
            pl.when(has_down)(lambda: down(index, source).start())
            to_peer(index, source).start()
            to_sibling(index, y, source).start()

        if hop == 1:
            for i in range(4):
                local[i].wait()
        project(hop - 1)

        @pl.when(c >= hop)
        def _():
            arrived(c - hop, peer)
            to_sibling(c - hop, 1 - y, block(c - hop, peer)).start()

        @pl.when(c + hop < ctx_size)
        def _():
            arrived(c + hop, peer)
            to_sibling(c + hop, 1 - y, block(c + hop, peer)).start()

    project(ctx_size - 1)

    score_scale = 1.0 / math.sqrt(HEAD)

    def context_copy(index):
        return remote(
            context_out.at[index],
            context_in.at[c],
            ctx_send.at[index],
            ctx_recv.at[c],
            ctx=index,
        )

    for place in reversed(range(ctx_size)):
        index = pick(order, c, place)
        here = pl.ds(pl.multiple_of(index * rows, 16), rows)
        scores = (
            lax.dot_general(
                q_all[here, :],
                k_all[...],
                (((1,), (1,)), ((), ())),
                preferred_element_type=jnp.float32,
            )
            * score_scale
        )
        weights = jnp.exp(scores - jnp.max(scores, axis=-1, keepdims=True))
        denominator = jnp.sum(weights, axis=-1, keepdims=True)
        weighted = jnp.dot(
            weights.astype(jnp.bfloat16), v_all[...], preferred_element_type=jnp.float32
        )
        context = (weighted / denominator).astype(jnp.bfloat16)
        if place:
            context_out[index] = context
            context_copy(index).start()
        else:
            context_in[c] = context

    local[4].wait()
    for hop in range(1, ctx_size):
        index = (c + hop) % ctx_size
        remote(
            context_out.at[index], context_in.at[index], ctx_send.at[index], ctx_recv.at[index], ctx=index
        ).wait_recv()

    def chunk(step):
        return pl.ds(step * step_rows, step_rows)

    mine = pl.ds(2 * k, 2)
    others = pl.ds(2 * (1 - k), 2)

    def stage(kind, step, source, target, device):
        return remote(
            source, target, stage_send.at[kind, step], stage_recv.at[kind, step], tp=device
        )

    def pair_copy(step):
        return stage(0, step, part16.at[others, chunk(step)], pair_in.at[:, chunk(step)], sibling)

    def peer_copy(step):
        return stage(1, step, pair_sum.at[:, chunk(step)], peer_in.at[:, chunk(step)], peer)

    def middle_copy(step, half):
        ref = middle.at[half, chunk(step)]
        return stage(2, step, ref, ref, sibling)

    for step in range(ROW_CHUNKS):
        terms = sum(
            jnp.dot(
                context_in[head, chunk(step), :HEAD],
                w_out[head * HEAD : (head + 1) * HEAD, :],
                preferred_element_type=jnp.float32,
            )
            for head in range(ctx_size)
        )
        for i in range(tp_size):
            piece = terms[:, i * cols : (i + 1) * cols]
            part32[i, chunk(step), :] = piece
            part16[i, chunk(step), :] = piece.astype(jnp.bfloat16)
        pair_copy(step).start()
    for step in range(ROW_CHUNKS):
        pair_copy(step).wait_recv()
        pair_sum[:, chunk(step), :] = (
            part32[mine, chunk(step), :] + pair_in[:, chunk(step), :].astype(jnp.float32)
        ).astype(jnp.bfloat16)
        peer_copy(step).start()

    for i in range(5, 9):
        local[i].wait()
    taps32[...] = taps[...].astype(jnp.float32)

    def halo_up():
        return remote(
            glu16.at[pl.ds(rows - HALO, HALO)], halo_low, halo_send.at[0], halo_recv.at[0], ctx=c + 1
        )

    def halo_down():
        return remote(glu16.at[pl.ds(0, HALO)], halo_high, halo_send.at[1], halo_recv.at[1], ctx=c - 1)

    for step in range(ROW_CHUNKS):
        peer_copy(step).wait_recv()
        own = pl.ds(pl.multiple_of(c * rows + step * step_rows, 16), step_rows)
        summed = pair_sum[:, chunk(step), :].astype(jnp.float32) + peer_in[
            :, chunk(step), :
        ].astype(jnp.float32)
        middle[mine, chunk(step), :] = (
            gathered[mine, own, :].astype(jnp.float32) + summed
        ).astype(jnp.bfloat16)
        middle_copy(step, mine).start()
        middle_copy(step, others).wait_recv()

        def store(part, value):
            normed[chunk(step), part * cols : (part + 1) * cols] = value

        norm_rows(
            [middle[i, chunk(step), :].astype(jnp.float32) for i in range(tp_size)],
            conv_gain[...],
            store,
        )
        halves = jnp.dot(normed[chunk(step), :], w_glu[...], preferred_element_type=jnp.float32)
        glu = (halves[:, :cols] * jax.nn.sigmoid(halves[:, cols:])).astype(jnp.bfloat16)
        glu16[chunk(step), :] = glu
        padded[HALO + step * step_rows : HALO + (step + 1) * step_rows, :] = glu.astype(jnp.float32)
        if step == 0:
            pl.when(has_down)(lambda: halo_down().start())
        if step == ROW_CHUNKS - 1:
            pl.when(has_up)(lambda: halo_up().start())

    padded[0:HALO, :] = jnp.zeros((HALO, cols), jnp.float32)
    padded[HALO + rows :, :] = jnp.zeros((HALO, cols), jnp.float32)

    @pl.when(has_down)
    def _():
        halo_up().wait_recv()
        padded[0:HALO, :] = halo_low[...].astype(jnp.float32)

    @pl.when(has_up)
    def _():
        halo_down().wait_recv()
        padded[HALO + rows :, :] = halo_high[...].astype(jnp.float32)

    def conv_pair(step):
        return stage(
            3, step, conv16.at[others, chunk(step)], conv_pair_in.at[:, chunk(step)], sibling
        )

    def conv_peer(step):
        return stage(4, step, conv_send.at[chunk(step)], conv_peer_in.at[chunk(step)], peer)

    tap_count = taps32.shape[0]
    first = HALO - tap_count // 2
    for step in range(ROW_CHUNKS):
        for lane in range(0, cols, 128):
            lanes = slice(lane, lane + 128)
            total = jnp.zeros((step_rows, 128), jnp.float32)
            for tap in range(tap_count):
                at = step * step_rows + first + tap
                total = total + padded[at : at + step_rows, lanes] * taps32[tap : tap + 1, lanes]
            total = total + depth_b[:, lanes]
            act[chunk(step), lanes] = (total / (1.0 + jnp.exp(-total))).astype(jnp.bfloat16)
        terms = jnp.dot(act[chunk(step), :], w_proj[...], preferred_element_type=jnp.float32)
        for i in range(tp_size):
            piece = terms[:, i * cols : (i + 1) * cols]
            slot = (i % 2) * 2 + i // 2
            conv32[slot, chunk(step), :] = piece
            conv16[slot, chunk(step), :] = piece.astype(jnp.bfloat16)
        conv_pair(step).start()
    for step in range(ROW_CHUNKS):
        conv_pair(step).wait_recv()
        conv_send[chunk(step), :] = (
            conv32[2 * k + 1 - y, chunk(step), :]
            + conv_pair_in[1 - y, chunk(step), :].astype(jnp.float32)
        ).astype(jnp.bfloat16)
        conv_peer(step).start()
        conv_keep[chunk(step), :] = (
            conv32[2 * k + y, chunk(step), :]
            + conv_pair_in[y, chunk(step), :].astype(jnp.float32)
            + middle[t, chunk(step), :].astype(jnp.float32)
        )
    for step in range(ROW_CHUNKS):
        conv_peer(step).wait_recv()
        out[chunk(step), :] = (
            conv_keep[chunk(step), :] + conv_peer_in[chunk(step), :].astype(jnp.float32)
        ).astype(jnp.bfloat16)

    pl.when(has_up)(lambda: up(c, frames).wait_send())
    pl.when(has_down)(lambda: down(c, frames).wait_send())
    to_peer(c, frames).wait_send()
    to_sibling(c, y, frames).wait_send()
    to_sibling(c, 1 - y, block(c, peer)).wait_send()
    for hop in range(1, ctx_size):

        @pl.when(c >= hop)
        def _():
            index = c - hop
            source = block(index, t)
            pl.when(has_up)(lambda: up(index, source).wait_send())
            to_peer(index, source).wait_send()
            to_sibling(index, y, source).wait_send()
            to_sibling(index, 1 - y, block(index, peer)).wait_send()

        @pl.when(c + hop < ctx_size)
        def _():
            index = c + hop
            source = block(index, t)
            pl.when(has_down)(lambda: down(index, source).wait_send())
            to_peer(index, source).wait_send()
            to_sibling(index, y, source).wait_send()
            to_sibling(index, 1 - y, block(index, peer)).wait_send()

        context_copy((c + hop) % ctx_size).wait_send()
    for step in range(ROW_CHUNKS):
        pair_copy(step).wait_send()
        peer_copy(step).wait_send()
        middle_copy(step, mine).wait_send()
        conv_pair(step).wait_send()
        conv_peer(step).wait_send()
    pl.when(has_up)(lambda: halo_up().wait_send())
    pl.when(has_down)(lambda: halo_down().wait_send())


def fused(
    ctx_size,
    tp_size,
    frames,
    attn_gain,
    query_key_value,
    out_weight,
    conv_gain,
    glu_weight,
    depth_kernel,
    depth_bias,
    proj_weight,
):
    rows, cols = frames.shape
    width = cols * tp_size
    all_rows = rows * ctx_size
    taps = depth_kernel.shape[0]
    wide, narrow = jnp.float32, jnp.bfloat16
    vmem = pl.BlockSpec(memory_space=pltpu.VMEM)
    away = pl.BlockSpec(memory_space=pl.ANY)
    dma = pltpu.SemaphoreType.DMA
    return pl.pallas_call(
        functools.partial(fused_kernel, ctx_size, tp_size),
        out_shape=jax.ShapeDtypeStruct((rows, cols), narrow),
        in_specs=[away, vmem, away, away, vmem, away, away, vmem, away],
        out_specs=vmem,
        scratch_shapes=[
            pltpu.VMEM((width, 3 * WINDOW), narrow),
            pltpu.VMEM((cols, width), narrow),
            pltpu.VMEM((width, 2 * cols), narrow),
            pltpu.VMEM((cols, width), narrow),
            pltpu.VMEM((taps, cols), narrow),
            pltpu.VMEM((taps, cols), wide),
            pltpu.VMEM((tp_size, all_rows, cols), narrow),
            pltpu.VMEM((rows, width), narrow),
            pltpu.VMEM((all_rows, WINDOW), narrow),
            pltpu.VMEM((all_rows, WINDOW), narrow),
            pltpu.VMEM((all_rows, 128), narrow),
            pltpu.VMEM((ctx_size, rows, 128), narrow),
            pltpu.VMEM((ctx_size, rows, 128), narrow),
            pltpu.VMEM((tp_size, rows, cols), wide),
            pltpu.VMEM((tp_size, rows, cols), narrow),
            pltpu.VMEM((2, rows, cols), narrow),
            pltpu.VMEM((2, rows, cols), narrow),
            pltpu.VMEM((2, rows, cols), narrow),
            pltpu.VMEM((tp_size, rows, cols), narrow),
            pltpu.VMEM((rows, cols), narrow),
            pltpu.VMEM((HALO, cols), narrow),
            pltpu.VMEM((HALO, cols), narrow),
            pltpu.VMEM((rows + 2 * HALO, cols), wide),
            pltpu.VMEM((rows, cols), narrow),
            pltpu.VMEM((tp_size, rows, cols), wide),
            pltpu.VMEM((tp_size, rows, cols), narrow),
            pltpu.VMEM((2, rows, cols), narrow),
            pltpu.VMEM((rows, cols), wide),
            pltpu.VMEM((rows, cols), narrow),
            pltpu.VMEM((rows, cols), narrow),
            dma((9,)),
            dma((ctx_size, tp_size)),
            dma((ctx_size, 2)),
            dma((ctx_size,)),
            dma((ctx_size,)),
            dma((ctx_size,)),
            dma((ctx_size,)),
            dma((ctx_size,)),
            dma((5, ROW_CHUNKS)),
            dma((5, ROW_CHUNKS)),
            dma((2,)),
            dma((2,)),
        ],
        compiler_params=pltpu.CompilerParams(
            collective_id=0, has_side_effects=True, vmem_limit_bytes=48 * 1024 * 1024
        ),
    )(
        frames,
        attn_gain.reshape(1, -1),
        query_key_value,
        out_weight,
        conv_gain.reshape(1, -1),
        glu_weight,
        depth_kernel,
        depth_bias.reshape(1, -1),
        proj_weight,
    )


def solution(mesh):
    in_specs = (
        P(("batch", "ctx"), "tp"),
        P(),
        P(None, None, "tp"),
        P("tp", None),
        P(),
        P(None, None, "tp"),
        P(None, "tp"),
        P("tp"),
        P("tp", None),
    )
    out_specs = P(("batch", "ctx"), "tp")
    ctx_size, tp_size = mesh.shape["ctx"], mesh.shape["tp"]

    def body(frames, attn_gain, query_key_value, *rest):
        one_head_each = ctx_size * HEAD == query_key_value.shape[2]
        if tp_size == 4 and one_head_each and frames.shape[0] % (16 * ROW_CHUNKS) == 0:
            return fused(ctx_size, tp_size, frames, attn_gain, query_key_value, *rest)
        return per_device(frames, attn_gain, query_key_value, *rest)

    return jax.shard_map(
        body, mesh=mesh, in_specs=in_specs, out_specs=out_specs, check_vma=False
    )
```

```python
import functools
import math

import jax
import jax.numpy as jnp
from jax import lax
from jax.experimental import pallas as pl
from jax.experimental.pallas import tpu as pltpu
from jax.sharding import PartitionSpec as P

HEAD = 96
HALO = 16
ROW_CHUNKS = 2
PARTS = 2
WINDOW = 256
MESH = pl.DeviceIdType.MESH


def layer_norm(inputs, gain):
    inputs = inputs.astype(jnp.float32)
    average = jnp.mean(inputs, axis=-1, keepdims=True)
    centered = inputs - average
    variance = jnp.mean(centered * centered, axis=-1, keepdims=True)
    return (centered * lax.rsqrt(variance + 1e-05) * gain).astype(jnp.bfloat16)


def depthwise(padded, kernel, bias, count):
    convolved = jnp.zeros((count, padded.shape[1]), jnp.float32)
    for kernel_tap in range(kernel.shape[0]):
        convolved = convolved + padded[kernel_tap : kernel_tap + count].astype(
            jnp.float32
        ) * kernel[kernel_tap].astype(jnp.float32)
    return jax.nn.silu(convolved + bias).astype(jnp.bfloat16)


def per_device(
    frames,
    attn_gain,
    query_key_value,
    out_weight,
    conv_gain,
    glu_weight,
    depth_kernel,
    depth_bias,
    proj_weight,
):
    frame_rows = frames.shape[0]
    local_cols = frames.shape[1]
    heads_here = query_key_value.shape[2] // HEAD
    whole_rows = lax.all_gather(frames, "tp", axis=1, tiled=True)
    normed = layer_norm(whole_rows, attn_gain)
    projected = jnp.einsum(
        "td,gdc->gtc", normed, query_key_value, preferred_element_type=jnp.float32
    ).astype(jnp.bfloat16)
    score_scale = 1.0 / math.sqrt(HEAD)
    query_heads = projected[0].reshape(frame_rows, heads_here, HEAD)
    initial = (
        jnp.full((heads_here, frame_rows), -1e30, jnp.float32),
        jnp.zeros((heads_here, frame_rows), jnp.float32),
        jnp.zeros((frame_rows, heads_here, HEAD), jnp.float32),
    )
    pieces = (
        lax.all_gather(projected[1], "ctx", axis=0, tiled=True),
        lax.all_gather(projected[2], "ctx", axis=0, tiled=True),
    )
    key_count = pieces[0].shape[0]
    block_len = 1024 if key_count > 1024 and key_count % 1024 == 0 else key_count
    key_blocks = pieces[0].reshape(key_count // block_len, block_len, heads_here, HEAD)
    value_blocks = pieces[1].reshape(key_count // block_len, block_len, heads_here, HEAD)

    def one_block(running, pieces_now):
        running_max, denominator, weighted = running
        key_block, value_block = pieces_now
        scores = (
            jnp.einsum("qhd,khd->hqk", query_heads, key_block, preferred_element_type=jnp.float32)
            * score_scale
        )
        new_max = jnp.maximum(running_max, jnp.max(scores, axis=-1))
        weights = jnp.exp(scores - new_max[:, :, None])
        rescale = jnp.exp(running_max - new_max)
        denominator = denominator * rescale + jnp.sum(weights, axis=-1)
        added = jnp.einsum(
            "hqk,khd->qhd",
            weights.astype(jnp.bfloat16),
            value_block,
            preferred_element_type=jnp.float32,
        )
        weighted = weighted * jnp.transpose(rescale)[:, :, None] + added
        return ((new_max, denominator, weighted), None)

    result, _ = lax.scan(one_block, initial, (key_blocks, value_blocks))
    running_max, denominator, weighted = result
    context = (
        (weighted / jnp.transpose(denominator)[:, :, None])
        .reshape(frame_rows, local_cols)
        .astype(jnp.bfloat16)
    )
    attn_terms = jnp.dot(context, out_weight, preferred_element_type=jnp.float32)
    summed = lax.psum(attn_terms.astype(jnp.bfloat16), "tp").astype(jnp.float32)
    middle_whole = (whole_rows.astype(jnp.float32) + summed).astype(jnp.bfloat16)
    middle = lax.dynamic_slice_in_dim(
        middle_whole, lax.axis_index("tp") * local_cols, local_cols, 1
    )
    normed_conv = layer_norm(middle_whole, conv_gain)
    halves = jnp.einsum("td,gdc->gtc", normed_conv, glu_weight, preferred_element_type=jnp.float32)
    glu = (halves[0] * jax.nn.sigmoid(halves[1])).astype(jnp.bfloat16)
    reach = depth_kernel.shape[0] // 2
    regrouped = lax.all_to_all(glu, "ctx", split_axis=1, concat_axis=0, tiled=True)
    group_cols = regrouped.shape[1]
    offset_cols = lax.axis_index("ctx") * group_cols
    kernel_part = lax.dynamic_slice_in_dim(depth_kernel, offset_cols, group_cols, 1)
    bias_part = lax.dynamic_slice_in_dim(depth_bias, offset_cols, group_cols, 0)
    padded = jnp.pad(regrouped, ((reach, reach), (0, 0)))
    activated_part = depthwise(padded, kernel_part, bias_part, regrouped.shape[0])
    activated = lax.all_to_all(activated_part, "ctx", split_axis=0, concat_axis=1, tiled=True)
    conv_terms = jnp.dot(activated, proj_weight, preferred_element_type=jnp.float32)
    conv_sum = lax.psum_scatter(
        conv_terms.astype(jnp.bfloat16), "tp", scatter_dimension=1, tiled=True
    ).astype(jnp.float32)
    return (middle.astype(jnp.float32) + conv_sum).astype(jnp.bfloat16)


def pick(table, row, column):
    value = 0
    for index, line in enumerate(table):
        value = value + jnp.where(row == index, line[column], 0)
    return value


def norm_rows(parts, gain, store):
    width = sum(part.shape[-1] for part in parts)
    total = sum(jnp.sum(part, axis=-1, keepdims=True) for part in parts)
    average = total / width
    centered = [part - average for part in parts]
    squares = sum(jnp.sum(part * part, axis=-1, keepdims=True) for part in centered)
    scale = lax.rsqrt(squares / width + 1e-05)
    start = 0
    for index, part in enumerate(centered):
        stop = start + part.shape[-1]
        store(index, (part * scale * gain[:, start:stop]).astype(jnp.bfloat16))
        start = stop


def fused_kernel(
    ctx_size,
    tp_size,
    frames,
    attn_gain,
    qkv,
    out_w,
    conv_gain,
    glu_w,
    depth_k,
    depth_b,
    proj_w,
    out,
    w_qkv,
    w_out,
    w_glu,
    w_proj,
    taps,
    taps32,
    attn_scale,
    conv_scale,
    bias,
    gathered,
    normed,
    q_all,
    k_all,
    v_all,
    context_out,
    context_in,
    part32,
    part16,
    pair_in,
    pair_sum,
    peer_in,
    middle,
    glu16,
    halo_low,
    halo_high,
    padded,
    act,
    conv32,
    conv16,
    conv_pair_in,
    conv_keep,
    conv_send,
    conv_peer_in,
    local_sem,
    gather_recv,
    sib_send,
    peer_send,
    up_send,
    down_send,
    ctx_send,
    ctx_recv,
    stage_send,
    stage_recv,
    halo_send,
    halo_recv,
):
    c = lax.axis_index("ctx")
    t = lax.axis_index("tp")
    y = t // 2
    k = t % 2
    sibling = y * 2 + (1 - k)
    peer = (1 - y) * 2 + k
    diagonal = (1 - y) * 2 + (1 - k)
    rows, cols = frames.shape
    step_rows = rows // ROW_CHUNKS

    def remote(source, target, send, receive, **device):
        return pltpu.make_async_remote_copy(
            src_ref=source,
            dst_ref=target,
            send_sem=send,
            recv_sem=receive,
            device_id=device,
            device_id_type=MESH,
        )

    first_col = c * HEAD
    window = jnp.minimum(first_col // 128, (cols - WINDOW) // 128)
    shift = first_col - window * 128
    window_cols = pl.ds(pl.multiple_of(window * 128, 128), WINDOW)

    part_rows = rows // PARTS

    def block(ctx_index, tp_index, part=None):
        if part is None:
            at = pl.ds(pl.multiple_of(ctx_index * rows, 16), rows)
        else:
            at = pl.ds(pl.multiple_of(ctx_index * rows + part * part_rows, 16), part_rows)
        return gathered.at[tp_index, at]

    local = [pltpu.make_async_copy(frames, block(c, t), local_sem.at[0])]
    for i in range(3):
        local.append(
            pltpu.make_async_copy(
                qkv.at[i, :, window_cols],
                w_qkv.at[:, pl.ds(i * WINDOW, WINDOW)],
                local_sem.at[1 + i],
            )
        )
    local.append(pltpu.make_async_copy(out_w, w_out, local_sem.at[4]))
    for i in range(2):
        local.append(
            pltpu.make_async_copy(
                glu_w.at[i], w_glu.at[:, pl.ds(i * cols, cols)], local_sem.at[5 + i]
            )
        )
    local.append(pltpu.make_async_copy(proj_w, w_proj, local_sem.at[7]))
    local.append(pltpu.make_async_copy(depth_k, taps, local_sem.at[8]))
    local.append(pltpu.make_async_copy(conv_gain, conv_scale, local_sem.at[9]))
    local.append(pltpu.make_async_copy(depth_b, bias, local_sem.at[10]))
    local.insert(4, pltpu.make_async_copy(attn_gain, attn_scale, local_sem.at[11]))

    barrier = pltpu.get_barrier_semaphore()
    for other in (sibling, peer):
        pl.semaphore_signal(barrier, inc=1, device_id={"tp": other}, device_id_type=MESH)
    for hop in range(1, ctx_size):
        pl.semaphore_signal(
            barrier, inc=1, device_id={"ctx": (c + hop) % ctx_size}, device_id_type=MESH
        )
    for copy in local:
        copy.start()
    pl.semaphore_wait(barrier, 2 + ctx_size - 1)

    def own_part(part):
        return frames.at[pl.ds(part * part_rows, part_rows)]

    def to_peer(index, part, source):
        return remote(
            source,
            block(index, t, part),
            peer_send.at[index, part],
            gather_recv.at[index, t, part],
            tp=peer,
        )

    def to_sibling(index, half, part, source):
        owner = half * 2 + k
        return remote(
            source,
            block(index, owner, part),
            sib_send.at[index, half, part],
            gather_recv.at[index, owner, part],
            tp=sibling,
        )

    def up(index, part, source):
        return remote(
            source,
            block(index, t, part),
            up_send.at[index, part],
            gather_recv.at[index, t, part],
            ctx=c + 1,
        )

    def down(index, part, source):
        return remote(
            source,
            block(index, t, part),
            down_send.at[index, part],
            gather_recv.at[index, t, part],
            ctx=c - 1,
        )

    def arrived(index, owner, part):
        here = block(index, owner, part)
        remote(
            here, here, peer_send.at[index, part], gather_recv.at[index, owner, part], tp=peer
        ).wait_recv()

    has_up = c + 1 < ctx_size
    has_down = c > 0

    for part in range(PARTS):
        source = own_part(part)
        pl.when(has_up)(lambda: up(c, part, source).start())
        pl.when(has_down)(lambda: down(c, part, source).start())
        to_peer(c, part, source).start()
        to_sibling(c, y, part, source).start()

    order = []
    for place in range(ctx_size):
        line = [place]
        for hop in range(1, ctx_size):
            line += [i for i in (place - hop, place + hop) if 0 <= i < ctx_size]
        order.append(line)

    key_lane = lax.broadcasted_iota(jnp.int32, (rows, WINDOW), 1)
    in_head = (key_lane >= shift) & (key_lane < shift + HEAD)
    select_row = lax.broadcasted_iota(jnp.int32, (WINDOW, 128), 0)
    select_col = lax.broadcasted_iota(jnp.int32, (WINDOW, 128), 1)
    select = ((select_row == select_col + shift) & (select_col < HEAD)).astype(jnp.bfloat16)

    def project(place):
        index = pick(order, c, place)
        for part in range(PARTS):
            arrived(index, sibling, part)
            arrived(index, diagonal, part)
        start = pl.multiple_of(index * rows, 16)
        sub = rows // 4

        def norm_step(step, carry):
            at = pl.ds(pl.multiple_of(start + step * sub, 16), sub)
            to = pl.ds(pl.multiple_of(step * sub, 16), sub)

            def store(part, value):
                normed[to, part * cols : (part + 1) * cols] = value

            norm_rows(
                [gathered[i, at, :].astype(jnp.float32) for i in range(tp_size)],
                attn_scale[...].reshape(1, -1),
                store,
            )
            return carry

        lax.fori_loop(0, 4, norm_step, 0)
        here = pl.ds(start, rows)
        projected = jnp.dot(normed[...], w_qkv[...], preferred_element_type=jnp.float32)
        q_all[here, :] = jnp.where(in_head, projected[:, :WINDOW], 0.0).astype(jnp.bfloat16)
        k_all[here, :] = projected[:, WINDOW : 2 * WINDOW].astype(jnp.bfloat16)
        v_all[here, :] = jnp.dot(
            projected[:, 2 * WINDOW :].astype(jnp.bfloat16),
            select,
            preferred_element_type=jnp.float32,
        ).astype(jnp.bfloat16)

    def pass_on(hop):
        for part in range(PARTS):

            @pl.when(c >= hop)
            def _():
                index = c - hop
                arrived(index, t, part)
                source = block(index, t, part)
                pl.when(has_up)(lambda: up(index, part, source).start())
                to_peer(index, part, source).start()
                to_sibling(index, y, part, source).start()

            @pl.when(c + hop < ctx_size)
            def _():
                index = c + hop
                arrived(index, t, part)
                source = block(index, t, part)
                pl.when(has_down)(lambda: down(index, part, source).start())
                to_peer(index, part, source).start()
                to_sibling(index, y, part, source).start()

    def from_peer(place):
        index = pick(order, c, place)
        for part in range(PARTS):
            arrived(index, peer, part)
            to_sibling(index, 1 - y, part, block(index, peer, part)).start()

    pass_on(1)
    from_peer(0)
    pass_on(2)
    from_peer(1)
    for i in range(5):
        local[i].wait()
    project(0)
    for place in range(2, ctx_size):
        last = place == ctx_size - 1
        if not last:
            pass_on(place + 1)
        else:
            project(place - 1)
        from_peer(place)
        if not last:
            project(place - 1)
    project(ctx_size - 1)

    score_scale = 1.0 / math.sqrt(HEAD)

    def context_copy(index):
        return remote(
            context_out.at[index],
            context_in.at[c],
            ctx_send.at[index],
            ctx_recv.at[c],
            ctx=index,
        )

    for place in reversed(range(ctx_size)):
        index = pick(order, c, place)
        here = pl.ds(pl.multiple_of(index * rows, 16), rows)
        scores = (
            lax.dot_general(
                q_all[here, :],
                k_all[...],
                (((1,), (1,)), ((), ())),
                preferred_element_type=jnp.float32,
            )
            * score_scale
        )
        weights = jnp.exp(scores - jnp.max(scores, axis=-1, keepdims=True))
        denominator = jnp.sum(weights, axis=-1, keepdims=True)
        weighted = jnp.dot(
            weights.astype(jnp.bfloat16), v_all[...], preferred_element_type=jnp.float32
        )
        context = (weighted / denominator).astype(jnp.bfloat16)
        if place:
            context_out[index] = context
            context_copy(index).start()
        else:
            context_in[c] = context

    local[5].wait()
    for hop in range(1, ctx_size):
        index = (c + hop) % ctx_size
        remote(
            context_out.at[index], context_in.at[index], ctx_send.at[index], ctx_recv.at[index], ctx=index
        ).wait_recv()

    def chunk(step):
        return pl.ds(step * step_rows, step_rows)

    mine = pl.ds(2 * k, 2)
    others = pl.ds(2 * (1 - k), 2)

    def stage(kind, step, source, target, device):
        return remote(
            source, target, stage_send.at[kind, step], stage_recv.at[kind, step], tp=device
        )

    def pair_copy(step):
        return stage(0, step, part16.at[others, chunk(step)], pair_in.at[:, chunk(step)], sibling)

    def peer_copy(step):
        return stage(1, step, pair_sum.at[:, chunk(step)], peer_in.at[:, chunk(step)], peer)

    def middle_copy(step, half):
        ref = middle.at[half, chunk(step)]
        return stage(2, step, ref, ref, sibling)

    for step in range(ROW_CHUNKS):
        terms = sum(
            jnp.dot(
                context_in[head, chunk(step), :HEAD],
                w_out[head * HEAD : (head + 1) * HEAD, :],
                preferred_element_type=jnp.float32,
            )
            for head in range(ctx_size)
        )
        for i in range(tp_size):
            piece = terms[:, i * cols : (i + 1) * cols]
            part32[i, chunk(step), :] = piece
            part16[i, chunk(step), :] = piece.astype(jnp.bfloat16)
        pair_copy(step).start()
    for step in range(ROW_CHUNKS):
        pair_copy(step).wait_recv()
        pair_sum[:, chunk(step), :] = (
            part32[mine, chunk(step), :] + pair_in[:, chunk(step), :].astype(jnp.float32)
        ).astype(jnp.bfloat16)
        peer_copy(step).start()

    for i in range(6, 12):
        local[i].wait()
    taps32[...] = taps[...].astype(jnp.float32)

    def halo_up():
        return remote(
            glu16.at[pl.ds(rows - HALO, HALO)], halo_low, halo_send.at[0], halo_recv.at[0], ctx=c + 1
        )

    def halo_down():
        return remote(glu16.at[pl.ds(0, HALO)], halo_high, halo_send.at[1], halo_recv.at[1], ctx=c - 1)

    for step in range(ROW_CHUNKS):
        peer_copy(step).wait_recv()
        own = pl.ds(pl.multiple_of(c * rows + step * step_rows, 16), step_rows)
        summed = pair_sum[:, chunk(step), :].astype(jnp.float32) + peer_in[
            :, chunk(step), :
        ].astype(jnp.float32)
        middle[mine, chunk(step), :] = (
            gathered[mine, own, :].astype(jnp.float32) + summed
        ).astype(jnp.bfloat16)
        middle_copy(step, mine).start()
        middle_copy(step, others).wait_recv()

        def store(part, value):
            normed[chunk(step), part * cols : (part + 1) * cols] = value

        norm_rows(
            [middle[i, chunk(step), :].astype(jnp.float32) for i in range(tp_size)],
            conv_scale[...].reshape(1, -1),
            store,
        )
        halves = jnp.dot(normed[chunk(step), :], w_glu[...], preferred_element_type=jnp.float32)
        glu = (halves[:, :cols] * jax.nn.sigmoid(halves[:, cols:])).astype(jnp.bfloat16)
        glu16[chunk(step), :] = glu
        padded[HALO + step * step_rows : HALO + (step + 1) * step_rows, :] = glu.astype(jnp.float32)
        if step == 0:
            pl.when(has_down)(lambda: halo_down().start())
        if step == ROW_CHUNKS - 1:
            pl.when(has_up)(lambda: halo_up().start())

    padded[0:HALO, :] = jnp.zeros((HALO, cols), jnp.float32)
    padded[HALO + rows :, :] = jnp.zeros((HALO, cols), jnp.float32)

    @pl.when(has_down)
    def _():
        halo_up().wait_recv()
        padded[0:HALO, :] = halo_low[...].astype(jnp.float32)

    @pl.when(has_up)
    def _():
        halo_down().wait_recv()
        padded[HALO + rows :, :] = halo_high[...].astype(jnp.float32)

    def conv_pair(step):
        return stage(
            3, step, conv16.at[others, chunk(step)], conv_pair_in.at[:, chunk(step)], sibling
        )

    def conv_peer(step):
        return stage(4, step, conv_send.at[chunk(step)], conv_peer_in.at[chunk(step)], peer)

    tap_count = taps32.shape[0]
    first = HALO - tap_count // 2
    for step in range(ROW_CHUNKS):
        for lane in range(0, cols, 128):
            lanes = slice(lane, lane + 128)
            total = jnp.zeros((step_rows, 128), jnp.float32)
            for tap in range(tap_count):
                at = step * step_rows + first + tap
                total = total + padded[at : at + step_rows, lanes] * taps32[tap : tap + 1, lanes]
            total = total + bias[lanes].reshape(1, -1)
            act[chunk(step), lanes] = (total / (1.0 + jnp.exp(-total))).astype(jnp.bfloat16)
        terms = jnp.dot(act[chunk(step), :], w_proj[...], preferred_element_type=jnp.float32)
        for i in range(tp_size):
            piece = terms[:, i * cols : (i + 1) * cols]
            slot = (i % 2) * 2 + i // 2
            conv32[slot, chunk(step), :] = piece
            conv16[slot, chunk(step), :] = piece.astype(jnp.bfloat16)
        conv_pair(step).start()
    for step in range(ROW_CHUNKS):
        conv_pair(step).wait_recv()
        conv_send[chunk(step), :] = (
            conv32[2 * k + 1 - y, chunk(step), :]
            + conv_pair_in[1 - y, chunk(step), :].astype(jnp.float32)
        ).astype(jnp.bfloat16)
        conv_peer(step).start()
        conv_keep[chunk(step), :] = (
            conv32[2 * k + y, chunk(step), :]
            + conv_pair_in[y, chunk(step), :].astype(jnp.float32)
            + middle[t, chunk(step), :].astype(jnp.float32)
        )
    for step in range(ROW_CHUNKS):
        conv_peer(step).wait_recv()
        out[chunk(step), :] = (
            conv_keep[chunk(step), :] + conv_peer_in[chunk(step), :].astype(jnp.float32)
        ).astype(jnp.bfloat16)

    for place in range(ctx_size):
        for part in range(PARTS):
            index = pick(order, c, place)
            source = block(index, t, part)
            pl.when(has_up & (index <= c))(lambda: up(index, part, source).wait_send())
            pl.when(has_down & (index >= c))(lambda: down(index, part, source).wait_send())
            to_peer(index, part, source).wait_send()
            to_sibling(index, y, part, source).wait_send()
            to_sibling(index, 1 - y, part, source).wait_send()
    for hop in range(1, ctx_size):
        context_copy((c + hop) % ctx_size).wait_send()
    for step in range(ROW_CHUNKS):
        pair_copy(step).wait_send()
        peer_copy(step).wait_send()
        middle_copy(step, mine).wait_send()
        conv_pair(step).wait_send()
        conv_peer(step).wait_send()
    pl.when(has_up)(lambda: halo_up().wait_send())
    pl.when(has_down)(lambda: halo_down().wait_send())


def fused(
    ctx_size,
    tp_size,
    frames,
    attn_gain,
    query_key_value,
    out_weight,
    conv_gain,
    glu_weight,
    depth_kernel,
    depth_bias,
    proj_weight,
):
    rows, cols = frames.shape
    width = cols * tp_size
    all_rows = rows * ctx_size
    taps = depth_kernel.shape[0]
    wide, narrow = jnp.float32, jnp.bfloat16
    vmem = pl.BlockSpec(memory_space=pltpu.VMEM)
    away = pl.BlockSpec(memory_space=pltpu.HBM)
    dma = pltpu.SemaphoreType.DMA
    return pl.pallas_call(
        functools.partial(fused_kernel, ctx_size, tp_size),
        out_shape=jax.ShapeDtypeStruct((rows, cols), narrow),
        in_specs=[away] * 9,
        out_specs=vmem,
        scratch_shapes=[
            pltpu.VMEM((width, 3 * WINDOW), narrow),
            pltpu.VMEM((cols, width), narrow),
            pltpu.VMEM((width, 2 * cols), narrow),
            pltpu.VMEM((cols, width), narrow),
            pltpu.VMEM((taps, cols), narrow),
            pltpu.VMEM((taps, cols), wide),
            pltpu.VMEM((width,), wide),
            pltpu.VMEM((width,), wide),
            pltpu.VMEM((cols,), wide),
            pltpu.VMEM((tp_size, all_rows, cols), narrow),
            pltpu.VMEM((rows, width), narrow),
            pltpu.VMEM((all_rows, WINDOW), narrow),
            pltpu.VMEM((all_rows, WINDOW), narrow),
            pltpu.VMEM((all_rows, 128), narrow),
            pltpu.VMEM((ctx_size, rows, 128), narrow),
            pltpu.VMEM((ctx_size, rows, 128), narrow),
            pltpu.VMEM((tp_size, rows, cols), wide),
            pltpu.VMEM((tp_size, rows, cols), narrow),
            pltpu.VMEM((2, rows, cols), narrow),
            pltpu.VMEM((2, rows, cols), narrow),
            pltpu.VMEM((2, rows, cols), narrow),
            pltpu.VMEM((tp_size, rows, cols), narrow),
            pltpu.VMEM((rows, cols), narrow),
            pltpu.VMEM((HALO, cols), narrow),
            pltpu.VMEM((HALO, cols), narrow),
            pltpu.VMEM((rows + 2 * HALO, cols), wide),
            pltpu.VMEM((rows, cols), narrow),
            pltpu.VMEM((tp_size, rows, cols), wide),
            pltpu.VMEM((tp_size, rows, cols), narrow),
            pltpu.VMEM((2, rows, cols), narrow),
            pltpu.VMEM((rows, cols), wide),
            pltpu.VMEM((rows, cols), narrow),
            pltpu.VMEM((rows, cols), narrow),
            dma((12,)),
            dma((ctx_size, tp_size, PARTS)),
            dma((ctx_size, 2, PARTS)),
            dma((ctx_size, PARTS)),
            dma((ctx_size, PARTS)),
            dma((ctx_size, PARTS)),
            dma((ctx_size,)),
            dma((ctx_size,)),
            dma((5, ROW_CHUNKS)),
            dma((5, ROW_CHUNKS)),
            dma((2,)),
            dma((2,)),
        ],
        compiler_params=pltpu.CompilerParams(
            collective_id=0, has_side_effects=True, vmem_limit_bytes=62 * 1024 * 1024
        ),
    )(
        frames,
        attn_gain,
        query_key_value,
        out_weight,
        conv_gain,
        glu_weight,
        depth_kernel,
        depth_bias,
        proj_weight,
    )


def solution(mesh):
    in_specs = (
        P(("batch", "ctx"), "tp"),
        P(),
        P(None, None, "tp"),
        P("tp", None),
        P(),
        P(None, None, "tp"),
        P(None, "tp"),
        P("tp"),
        P("tp", None),
    )
    out_specs = P(("batch", "ctx"), "tp")
    ctx_size, tp_size = mesh.shape["ctx"], mesh.shape["tp"]

    def body(frames, attn_gain, query_key_value, *rest):
        one_head_each = ctx_size * HEAD == query_key_value.shape[2]
        even = frames.shape[0] % (16 * ROW_CHUNKS * PARTS) == 0
        if tp_size == 4 and one_head_each and ctx_size > 2 and even:
            return fused(ctx_size, tp_size, frames, attn_gain, query_key_value, *rest)
        return per_device(frames, attn_gain, query_key_value, *rest)

    return jax.shard_map(
        body, mesh=mesh, in_specs=in_specs, out_specs=out_specs, check_vma=False
    )
```

```python
import functools
import math

import jax
import jax.numpy as jnp
from jax import lax
from jax.experimental import pallas as pl
from jax.experimental.pallas import tpu as pltpu
from jax.sharding import PartitionSpec as P

HEAD = 96
HALO = 16
ROW_CHUNKS = 2
PARTS = 2
WINDOW = 256
MESH = pl.DeviceIdType.MESH


def layer_norm(inputs, gain):
    inputs = inputs.astype(jnp.float32)
    average = jnp.mean(inputs, axis=-1, keepdims=True)
    centered = inputs - average
    variance = jnp.mean(centered * centered, axis=-1, keepdims=True)
    return (centered * lax.rsqrt(variance + 1e-05) * gain).astype(jnp.bfloat16)


def depthwise(padded, kernel, bias, count):
    convolved = jnp.zeros((count, padded.shape[1]), jnp.float32)
    for kernel_tap in range(kernel.shape[0]):
        convolved = convolved + padded[kernel_tap : kernel_tap + count].astype(
            jnp.float32
        ) * kernel[kernel_tap].astype(jnp.float32)
    return jax.nn.silu(convolved + bias).astype(jnp.bfloat16)


def per_device(
    frames,
    attn_gain,
    query_key_value,
    out_weight,
    conv_gain,
    glu_weight,
    depth_kernel,
    depth_bias,
    proj_weight,
):
    frame_rows = frames.shape[0]
    local_cols = frames.shape[1]
    heads_here = query_key_value.shape[2] // HEAD
    whole_rows = lax.all_gather(frames, "tp", axis=1, tiled=True)
    normed = layer_norm(whole_rows, attn_gain)
    projected = jnp.einsum(
        "td,gdc->gtc", normed, query_key_value, preferred_element_type=jnp.float32
    ).astype(jnp.bfloat16)
    score_scale = 1.0 / math.sqrt(HEAD)
    query_heads = projected[0].reshape(frame_rows, heads_here, HEAD)
    initial = (
        jnp.full((heads_here, frame_rows), -1e30, jnp.float32),
        jnp.zeros((heads_here, frame_rows), jnp.float32),
        jnp.zeros((frame_rows, heads_here, HEAD), jnp.float32),
    )
    pieces = (
        lax.all_gather(projected[1], "ctx", axis=0, tiled=True),
        lax.all_gather(projected[2], "ctx", axis=0, tiled=True),
    )
    key_count = pieces[0].shape[0]
    block_len = 1024 if key_count > 1024 and key_count % 1024 == 0 else key_count
    key_blocks = pieces[0].reshape(key_count // block_len, block_len, heads_here, HEAD)
    value_blocks = pieces[1].reshape(key_count // block_len, block_len, heads_here, HEAD)

    def one_block(running, pieces_now):
        running_max, denominator, weighted = running
        key_block, value_block = pieces_now
        scores = (
            jnp.einsum("qhd,khd->hqk", query_heads, key_block, preferred_element_type=jnp.float32)
            * score_scale
        )
        new_max = jnp.maximum(running_max, jnp.max(scores, axis=-1))
        weights = jnp.exp(scores - new_max[:, :, None])
        rescale = jnp.exp(running_max - new_max)
        denominator = denominator * rescale + jnp.sum(weights, axis=-1)
        added = jnp.einsum(
            "hqk,khd->qhd",
            weights.astype(jnp.bfloat16),
            value_block,
            preferred_element_type=jnp.float32,
        )
        weighted = weighted * jnp.transpose(rescale)[:, :, None] + added
        return ((new_max, denominator, weighted), None)

    result, _ = lax.scan(one_block, initial, (key_blocks, value_blocks))
    running_max, denominator, weighted = result
    context = (
        (weighted / jnp.transpose(denominator)[:, :, None])
        .reshape(frame_rows, local_cols)
        .astype(jnp.bfloat16)
    )
    attn_terms = jnp.dot(context, out_weight, preferred_element_type=jnp.float32)
    summed = lax.psum(attn_terms.astype(jnp.bfloat16), "tp").astype(jnp.float32)
    middle_whole = (whole_rows.astype(jnp.float32) + summed).astype(jnp.bfloat16)
    middle = lax.dynamic_slice_in_dim(
        middle_whole, lax.axis_index("tp") * local_cols, local_cols, 1
    )
    normed_conv = layer_norm(middle_whole, conv_gain)
    halves = jnp.einsum("td,gdc->gtc", normed_conv, glu_weight, preferred_element_type=jnp.float32)
    glu = (halves[0] * jax.nn.sigmoid(halves[1])).astype(jnp.bfloat16)
    reach = depth_kernel.shape[0] // 2
    regrouped = lax.all_to_all(glu, "ctx", split_axis=1, concat_axis=0, tiled=True)
    group_cols = regrouped.shape[1]
    offset_cols = lax.axis_index("ctx") * group_cols
    kernel_part = lax.dynamic_slice_in_dim(depth_kernel, offset_cols, group_cols, 1)
    bias_part = lax.dynamic_slice_in_dim(depth_bias, offset_cols, group_cols, 0)
    padded = jnp.pad(regrouped, ((reach, reach), (0, 0)))
    activated_part = depthwise(padded, kernel_part, bias_part, regrouped.shape[0])
    activated = lax.all_to_all(activated_part, "ctx", split_axis=0, concat_axis=1, tiled=True)
    conv_terms = jnp.dot(activated, proj_weight, preferred_element_type=jnp.float32)
    conv_sum = lax.psum_scatter(
        conv_terms.astype(jnp.bfloat16), "tp", scatter_dimension=1, tiled=True
    ).astype(jnp.float32)
    return (middle.astype(jnp.float32) + conv_sum).astype(jnp.bfloat16)


def pick(table, row, column):
    value = 0
    for index, line in enumerate(table):
        value = value + jnp.where(row == index, line[column], 0)
    return value


def norm_rows(parts, gain, store):
    width = sum(part.shape[-1] for part in parts)
    total = sum(jnp.sum(part, axis=-1, keepdims=True) for part in parts)
    average = total / width
    centered = [part - average for part in parts]
    squares = sum(jnp.sum(part * part, axis=-1, keepdims=True) for part in centered)
    scale = lax.rsqrt(squares / width + 1e-05)
    start = 0
    for index, part in enumerate(centered):
        stop = start + part.shape[-1]
        store(index, (part * scale * gain[:, start:stop]).astype(jnp.bfloat16))
        start = stop


def fused_kernel(
    ctx_size,
    tp_size,
    frames,
    attn_gain,
    qkv,
    out_w,
    conv_gain,
    glu_w,
    depth_k,
    depth_b,
    proj_w,
    out,
    w_qkv,
    w_out,
    w_glu,
    w_proj,
    taps,
    taps32,
    attn_scale,
    conv_scale,
    bias,
    gathered,
    normed,
    q_all,
    k_all,
    v_all,
    context_out,
    context_in,
    part32,
    part16,
    pair_in,
    pair_sum,
    peer_in,
    middle,
    glu16,
    halo_low,
    halo_high,
    padded,
    act,
    conv32,
    conv16,
    conv_pair_in,
    conv_keep,
    conv_send,
    conv_peer_in,
    local_sem,
    gather_recv,
    sib_send,
    peer_send,
    up_send,
    down_send,
    ctx_send,
    ctx_recv,
    stage_send,
    stage_recv,
    halo_send,
    halo_recv,
):
    c = lax.axis_index("ctx")
    t = lax.axis_index("tp")
    y = t // 2
    k = t % 2
    sibling = y * 2 + (1 - k)
    peer = (1 - y) * 2 + k
    diagonal = (1 - y) * 2 + (1 - k)
    rows, cols = frames.shape
    step_rows = rows // ROW_CHUNKS

    def remote(source, target, send, receive, **device):
        return pltpu.make_async_remote_copy(
            src_ref=source,
            dst_ref=target,
            send_sem=send,
            recv_sem=receive,
            device_id=device,
            device_id_type=MESH,
        )

    first_col = c * HEAD
    window = jnp.minimum(first_col // 128, (cols - WINDOW) // 128)
    shift = first_col - window * 128
    window_cols = pl.ds(pl.multiple_of(window * 128, 128), WINDOW)

    part_rows = rows // PARTS

    def block(ctx_index, tp_index, part=None):
        if part is None:
            at = pl.ds(pl.multiple_of(ctx_index * rows, 16), rows)
        else:
            at = pl.ds(pl.multiple_of(ctx_index * rows + part * part_rows, 16), part_rows)
        return gathered.at[tp_index, at]

    local = [pltpu.make_async_copy(frames, block(c, t), local_sem.at[0])]
    for i in range(3):
        local.append(
            pltpu.make_async_copy(
                qkv.at[i, :, window_cols],
                w_qkv.at[:, pl.ds(i * WINDOW, WINDOW)],
                local_sem.at[1 + i],
            )
        )
    local.append(pltpu.make_async_copy(out_w, w_out, local_sem.at[4]))
    for i in range(2):
        local.append(
            pltpu.make_async_copy(
                glu_w.at[i], w_glu.at[:, pl.ds(i * cols, cols)], local_sem.at[5 + i]
            )
        )
    local.append(pltpu.make_async_copy(proj_w, w_proj, local_sem.at[7]))
    local.append(pltpu.make_async_copy(depth_k, taps, local_sem.at[8]))
    local.append(pltpu.make_async_copy(conv_gain, conv_scale, local_sem.at[9]))
    local.append(pltpu.make_async_copy(depth_b, bias, local_sem.at[10]))
    local.insert(4, pltpu.make_async_copy(attn_gain, attn_scale, local_sem.at[11]))

    barrier = pltpu.get_barrier_semaphore()
    for other in (sibling, peer):
        pl.semaphore_signal(barrier, inc=1, device_id={"tp": other}, device_id_type=MESH)
    for hop in range(1, ctx_size):
        pl.semaphore_signal(
            barrier, inc=1, device_id={"ctx": (c + hop) % ctx_size}, device_id_type=MESH
        )
    for copy in local:
        copy.start()
    pl.semaphore_wait(barrier, 2 + ctx_size - 1)

    def own_part(part):
        return frames.at[pl.ds(part * part_rows, part_rows)]

    def to_peer(index, part, source):
        return remote(
            source,
            block(index, t, part),
            peer_send.at[index, part],
            gather_recv.at[index, t, part],
            tp=peer,
        )

    def to_sibling(index, half, part, source):
        owner = half * 2 + k
        return remote(
            source,
            block(index, owner, part),
            sib_send.at[index, half, part],
            gather_recv.at[index, owner, part],
            tp=sibling,
        )

    def up(index, part, source):
        return remote(
            source,
            block(index, t, part),
            up_send.at[index, part],
            gather_recv.at[index, t, part],
            ctx=c + 1,
        )

    def down(index, part, source):
        return remote(
            source,
            block(index, t, part),
            down_send.at[index, part],
            gather_recv.at[index, t, part],
            ctx=c - 1,
        )

    def arrived(index, owner, part):
        here = block(index, owner, part)
        remote(
            here, here, peer_send.at[index, part], gather_recv.at[index, owner, part], tp=peer
        ).wait_recv()

    has_up = c + 1 < ctx_size
    has_down = c > 0

    for part in range(PARTS):
        source = own_part(part)
        pl.when(has_up)(lambda: up(c, part, source).start())
        pl.when(has_down)(lambda: down(c, part, source).start())
        to_peer(c, part, source).start()
        to_sibling(c, y, part, source).start()

    order = []
    for place in range(ctx_size):
        line = [place]
        for hop in range(1, ctx_size):
            line += [i for i in (place - hop, place + hop) if 0 <= i < ctx_size]
        order.append(line)

    key_lane = lax.broadcasted_iota(jnp.int32, (rows, WINDOW), 1)
    in_head = (key_lane >= shift) & (key_lane < shift + HEAD)
    select_row = lax.broadcasted_iota(jnp.int32, (WINDOW, 128), 0)
    select_col = lax.broadcasted_iota(jnp.int32, (WINDOW, 128), 1)
    select = ((select_row == select_col + shift) & (select_col < HEAD)).astype(jnp.bfloat16)

    def project(place):
        index = pick(order, c, place)
        start = pl.multiple_of(index * rows, 16)
        sub = part_rows // 2
        for part in range(PARTS):
            arrived(index, sibling, part)
            arrived(index, diagonal, part)
            for step in range(2 * part, 2 * part + 2):
                at = pl.ds(pl.multiple_of(start + step * sub, 16), sub)

                def store(piece, value):
                    normed[pl.ds(step * sub, sub), piece * cols : (piece + 1) * cols] = value

                norm_rows(
                    [gathered[i, at, :].astype(jnp.float32) for i in range(tp_size)],
                    attn_scale[...].reshape(1, -1),
                    store,
                )
        here = pl.ds(start, rows)
        projected = jnp.dot(normed[...], w_qkv[...], preferred_element_type=jnp.float32)
        q_all[here, :] = jnp.where(in_head, projected[:, :WINDOW], 0.0).astype(jnp.bfloat16)
        k_all[here, :] = projected[:, WINDOW : 2 * WINDOW].astype(jnp.bfloat16)
        v_all[here, :] = jnp.dot(
            projected[:, 2 * WINDOW :].astype(jnp.bfloat16),
            select,
            preferred_element_type=jnp.float32,
        ).astype(jnp.bfloat16)

    def pass_on(hop):
        for part in range(PARTS):

            @pl.when(c >= hop)
            def _():
                index = c - hop
                arrived(index, t, part)
                source = block(index, t, part)
                pl.when(has_up)(lambda: up(index, part, source).start())
                to_peer(index, part, source).start()
                to_sibling(index, y, part, source).start()

            @pl.when(c + hop < ctx_size)
            def _():
                index = c + hop
                arrived(index, t, part)
                source = block(index, t, part)
                pl.when(has_down)(lambda: down(index, part, source).start())
                to_peer(index, part, source).start()
                to_sibling(index, y, part, source).start()

    def from_peer(place):
        index = pick(order, c, place)
        for part in range(PARTS):
            arrived(index, peer, part)
            to_sibling(index, 1 - y, part, block(index, peer, part)).start()

    pass_on(1)
    from_peer(0)
    pass_on(2)
    from_peer(1)
    for i in range(5):
        local[i].wait()
    project(0)
    for place in range(2, ctx_size):
        last = place == ctx_size - 1
        if not last:
            pass_on(place + 1)
        else:
            project(place - 1)
        from_peer(place)
        if not last:
            project(place - 1)
    project(ctx_size - 1)

    score_scale = 1.0 / math.sqrt(HEAD)

    def chunk(step):
        return pl.ds(step * step_rows, step_rows)

    def context_copy(index, step):
        return remote(
            context_out.at[index, chunk(step)],
            context_in.at[c, chunk(step)],
            ctx_send.at[index, step],
            ctx_recv.at[c, step],
            ctx=index,
        )

    def attend(step, place):
        index = pick(order, c, place)
        here = pl.ds(pl.multiple_of(index * rows + step * step_rows, 16), step_rows)
        scores = (
            lax.dot_general(
                q_all[here, :],
                k_all[...],
                (((1,), (1,)), ((), ())),
                preferred_element_type=jnp.float32,
            )
            * score_scale
        )
        weights = jnp.exp(scores - jnp.max(scores, axis=-1, keepdims=True))
        denominator = jnp.sum(weights, axis=-1, keepdims=True)
        weighted = jnp.dot(
            weights.astype(jnp.bfloat16), v_all[...], preferred_element_type=jnp.float32
        )
        context = (weighted / denominator).astype(jnp.bfloat16)
        if place:
            context_out[index, chunk(step), :] = context
            context_copy(index, step).start()
        else:
            context_in[c, chunk(step), :] = context

    for step in range(ROW_CHUNKS):
        for place in reversed(range(ctx_size)):
            attend(step, place)
    local[5].wait()

    mine = pl.ds(2 * k, 2)
    others = pl.ds(2 * (1 - k), 2)

    def stage(kind, step, source, target, device):
        return remote(
            source, target, stage_send.at[kind, step], stage_recv.at[kind, step], tp=device
        )

    def pair_copy(step):
        return stage(0, step, part16.at[others, chunk(step)], pair_in.at[:, chunk(step)], sibling)

    def peer_copy(step):
        return stage(1, step, pair_sum.at[:, chunk(step)], peer_in.at[:, chunk(step)], peer)

    def middle_copy(step, half):
        ref = middle.at[half, chunk(step)]
        return stage(2, step, ref, ref, sibling)

    for step in range(ROW_CHUNKS):
        for hop in range(1, ctx_size):
            index = (c + hop) % ctx_size
            here = context_in.at[index, chunk(step)]
            remote(here, here, ctx_send.at[index, step], ctx_recv.at[index, step], ctx=index).wait_recv()
        terms = sum(
            jnp.dot(
                context_in[head, chunk(step), :HEAD],
                w_out[head * HEAD : (head + 1) * HEAD, :],
                preferred_element_type=jnp.float32,
            )
            for head in range(ctx_size)
        )
        for i in range(tp_size):
            piece = terms[:, i * cols : (i + 1) * cols]
            part32[i, chunk(step), :] = piece
            part16[i, chunk(step), :] = piece.astype(jnp.bfloat16)
        pair_copy(step).start()
    for step in range(ROW_CHUNKS):
        pair_copy(step).wait_recv()
        pair_sum[:, chunk(step), :] = (
            part32[mine, chunk(step), :] + pair_in[:, chunk(step), :].astype(jnp.float32)
        ).astype(jnp.bfloat16)
        peer_copy(step).start()

    for i in range(6, 12):
        local[i].wait()
    taps32[...] = taps[...].astype(jnp.float32)

    def halo_up():
        return remote(
            glu16.at[pl.ds(rows - HALO, HALO)], halo_low, halo_send.at[0], halo_recv.at[0], ctx=c + 1
        )

    def halo_down():
        return remote(glu16.at[pl.ds(0, HALO)], halo_high, halo_send.at[1], halo_recv.at[1], ctx=c - 1)

    for step in range(ROW_CHUNKS):
        peer_copy(step).wait_recv()
        own = pl.ds(pl.multiple_of(c * rows + step * step_rows, 16), step_rows)
        summed = pair_sum[:, chunk(step), :].astype(jnp.float32) + peer_in[
            :, chunk(step), :
        ].astype(jnp.float32)
        middle[mine, chunk(step), :] = (
            gathered[mine, own, :].astype(jnp.float32) + summed
        ).astype(jnp.bfloat16)
        middle_copy(step, mine).start()
        middle_copy(step, others).wait_recv()

        def store(part, value):
            normed[chunk(step), part * cols : (part + 1) * cols] = value

        norm_rows(
            [middle[i, chunk(step), :].astype(jnp.float32) for i in range(tp_size)],
            conv_scale[...].reshape(1, -1),
            store,
        )
        halves = jnp.dot(normed[chunk(step), :], w_glu[...], preferred_element_type=jnp.float32)
        glu = (halves[:, :cols] * jax.nn.sigmoid(halves[:, cols:])).astype(jnp.bfloat16)
        glu16[chunk(step), :] = glu
        padded[HALO + step * step_rows : HALO + (step + 1) * step_rows, :] = glu.astype(jnp.float32)
        if step == 0:
            pl.when(has_down)(lambda: halo_down().start())
        if step == ROW_CHUNKS - 1:
            pl.when(has_up)(lambda: halo_up().start())

    def edge_low():
        padded[0:HALO, :] = jnp.zeros((HALO, cols), jnp.float32)

        @pl.when(has_down)
        def _():
            halo_up().wait_recv()
            padded[0:HALO, :] = halo_low[...].astype(jnp.float32)

    def edge_high():
        padded[HALO + rows :, :] = jnp.zeros((HALO, cols), jnp.float32)

        @pl.when(has_up)
        def _():
            halo_down().wait_recv()
            padded[HALO + rows :, :] = halo_high[...].astype(jnp.float32)

    def conv_pair(step):
        return stage(
            3, step, conv16.at[others, chunk(step)], conv_pair_in.at[:, chunk(step)], sibling
        )

    def conv_peer(step):
        return stage(4, step, conv_send.at[chunk(step)], conv_peer_in.at[chunk(step)], peer)

    tap_count = taps32.shape[0]
    first = HALO - tap_count // 2
    last_first = list(reversed(range(ROW_CHUNKS)))
    for step in last_first:
        if step == ROW_CHUNKS - 1:
            edge_high()
        if step == 0:
            edge_low()
        for lane in range(0, cols, 128):
            lanes = slice(lane, lane + 128)
            total = jnp.zeros((step_rows, 128), jnp.float32)
            for tap in range(tap_count):
                at = step * step_rows + first + tap
                total = total + padded[at : at + step_rows, lanes] * taps32[tap : tap + 1, lanes]
            total = total + bias[lanes].reshape(1, -1)
            act[chunk(step), lanes] = (total / (1.0 + jnp.exp(-total))).astype(jnp.bfloat16)
        terms = jnp.dot(act[chunk(step), :], w_proj[...], preferred_element_type=jnp.float32)
        for i in range(tp_size):
            piece = terms[:, i * cols : (i + 1) * cols]
            slot = (i % 2) * 2 + i // 2
            conv32[slot, chunk(step), :] = piece
            conv16[slot, chunk(step), :] = piece.astype(jnp.bfloat16)
        conv_pair(step).start()
    for step in last_first:
        conv_pair(step).wait_recv()
        conv_send[chunk(step), :] = (
            conv32[2 * k + 1 - y, chunk(step), :]
            + conv_pair_in[1 - y, chunk(step), :].astype(jnp.float32)
        ).astype(jnp.bfloat16)
        conv_peer(step).start()
        conv_keep[chunk(step), :] = (
            conv32[2 * k + y, chunk(step), :]
            + conv_pair_in[y, chunk(step), :].astype(jnp.float32)
            + middle[t, chunk(step), :].astype(jnp.float32)
        )
    for step in last_first:
        conv_peer(step).wait_recv()
        out[chunk(step), :] = (
            conv_keep[chunk(step), :] + conv_peer_in[chunk(step), :].astype(jnp.float32)
        ).astype(jnp.bfloat16)

    for place in range(ctx_size):
        for part in range(PARTS):
            index = pick(order, c, place)
            source = block(index, t, part)
            pl.when(has_up & (index <= c))(lambda: up(index, part, source).wait_send())
            pl.when(has_down & (index >= c))(lambda: down(index, part, source).wait_send())
            to_peer(index, part, source).wait_send()
            to_sibling(index, y, part, source).wait_send()
            to_sibling(index, 1 - y, part, source).wait_send()
    for hop in range(1, ctx_size):
        for step in range(ROW_CHUNKS):
            context_copy((c + hop) % ctx_size, step).wait_send()
    for step in range(ROW_CHUNKS):
        pair_copy(step).wait_send()
        peer_copy(step).wait_send()
        middle_copy(step, mine).wait_send()
        conv_pair(step).wait_send()
        conv_peer(step).wait_send()
    pl.when(has_up)(lambda: halo_up().wait_send())
    pl.when(has_down)(lambda: halo_down().wait_send())


def fused(
    ctx_size,
    tp_size,
    frames,
    attn_gain,
    query_key_value,
    out_weight,
    conv_gain,
    glu_weight,
    depth_kernel,
    depth_bias,
    proj_weight,
):
    rows, cols = frames.shape
    width = cols * tp_size
    all_rows = rows * ctx_size
    taps = depth_kernel.shape[0]
    wide, narrow = jnp.float32, jnp.bfloat16
    vmem = pl.BlockSpec(memory_space=pltpu.VMEM)
    away = pl.BlockSpec(memory_space=pltpu.HBM)
    dma = pltpu.SemaphoreType.DMA
    return pl.pallas_call(
        functools.partial(fused_kernel, ctx_size, tp_size),
        out_shape=jax.ShapeDtypeStruct((rows, cols), narrow),
        in_specs=[away] * 9,
        out_specs=vmem,
        scratch_shapes=[
            pltpu.VMEM((width, 3 * WINDOW), narrow),
            pltpu.VMEM((cols, width), narrow),
            pltpu.VMEM((width, 2 * cols), narrow),
            pltpu.VMEM((cols, width), narrow),
            pltpu.VMEM((taps, cols), narrow),
            pltpu.VMEM((taps, cols), wide),
            pltpu.VMEM((width,), wide),
            pltpu.VMEM((width,), wide),
            pltpu.VMEM((cols,), wide),
            pltpu.VMEM((tp_size, all_rows, cols), narrow),
            pltpu.VMEM((rows, width), narrow),
            pltpu.VMEM((all_rows, WINDOW), narrow),
            pltpu.VMEM((all_rows, WINDOW), narrow),
            pltpu.VMEM((all_rows, 128), narrow),
            pltpu.VMEM((ctx_size, rows, 128), narrow),
            pltpu.VMEM((ctx_size, rows, 128), narrow),
            pltpu.VMEM((tp_size, rows, cols), wide),
            pltpu.VMEM((tp_size, rows, cols), narrow),
            pltpu.VMEM((2, rows, cols), narrow),
            pltpu.VMEM((2, rows, cols), narrow),
            pltpu.VMEM((2, rows, cols), narrow),
            pltpu.VMEM((tp_size, rows, cols), narrow),
            pltpu.VMEM((rows, cols), narrow),
            pltpu.VMEM((HALO, cols), narrow),
            pltpu.VMEM((HALO, cols), narrow),
            pltpu.VMEM((rows + 2 * HALO, cols), wide),
            pltpu.VMEM((rows, cols), narrow),
            pltpu.VMEM((tp_size, rows, cols), wide),
            pltpu.VMEM((tp_size, rows, cols), narrow),
            pltpu.VMEM((2, rows, cols), narrow),
            pltpu.VMEM((rows, cols), wide),
            pltpu.VMEM((rows, cols), narrow),
            pltpu.VMEM((rows, cols), narrow),
            dma((12,)),
            dma((ctx_size, tp_size, PARTS)),
            dma((ctx_size, 2, PARTS)),
            dma((ctx_size, PARTS)),
            dma((ctx_size, PARTS)),
            dma((ctx_size, PARTS)),
            dma((ctx_size, ROW_CHUNKS)),
            dma((ctx_size, ROW_CHUNKS)),
            dma((5, ROW_CHUNKS)),
            dma((5, ROW_CHUNKS)),
            dma((2,)),
            dma((2,)),
        ],
        compiler_params=pltpu.CompilerParams(
            collective_id=0, has_side_effects=True, vmem_limit_bytes=62 * 1024 * 1024
        ),
    )(
        frames,
        attn_gain,
        query_key_value,
        out_weight,
        conv_gain,
        glu_weight,
        depth_kernel,
        depth_bias,
        proj_weight,
    )


def solution(mesh):
    in_specs = (
        P(("batch", "ctx"), "tp"),
        P(),
        P(None, None, "tp"),
        P("tp", None),
        P(),
        P(None, None, "tp"),
        P(None, "tp"),
        P("tp"),
        P("tp", None),
    )
    out_specs = P(("batch", "ctx"), "tp")
    ctx_size, tp_size = mesh.shape["ctx"], mesh.shape["tp"]

    def body(frames, attn_gain, query_key_value, *rest):
        one_head_each = ctx_size * HEAD == query_key_value.shape[2]
        even = frames.shape[0] % (16 * ROW_CHUNKS * PARTS) == 0
        if tp_size == 4 and one_head_each and ctx_size > 2 and even:
            return fused(ctx_size, tp_size, frames, attn_gain, query_key_value, *rest)
        return per_device(frames, attn_gain, query_key_value, *rest)

    return jax.shard_map(
        body, mesh=mesh, in_specs=in_specs, out_specs=out_specs, check_vma=False
    )
```

```python
import functools
import math

import jax
import jax.numpy as jnp
from jax import lax
from jax.experimental import pallas as pl
from jax.experimental.pallas import tpu as pltpu
from jax.sharding import PartitionSpec as P

HEAD = 96
HALO = 16
ROW_CHUNKS = 3
PARTS = 2
WINDOW = 256
MESH = pl.DeviceIdType.MESH


def layer_norm(inputs, gain):
    inputs = inputs.astype(jnp.float32)
    average = jnp.mean(inputs, axis=-1, keepdims=True)
    centered = inputs - average
    variance = jnp.mean(centered * centered, axis=-1, keepdims=True)
    return (centered * lax.rsqrt(variance + 1e-05) * gain).astype(jnp.bfloat16)


def depthwise(padded, kernel, bias, count):
    convolved = jnp.zeros((count, padded.shape[1]), jnp.float32)
    for kernel_tap in range(kernel.shape[0]):
        convolved = convolved + padded[kernel_tap : kernel_tap + count].astype(
            jnp.float32
        ) * kernel[kernel_tap].astype(jnp.float32)
    return jax.nn.silu(convolved + bias).astype(jnp.bfloat16)


def per_device(
    frames,
    attn_gain,
    query_key_value,
    out_weight,
    conv_gain,
    glu_weight,
    depth_kernel,
    depth_bias,
    proj_weight,
):
    frame_rows = frames.shape[0]
    local_cols = frames.shape[1]
    heads_here = query_key_value.shape[2] // HEAD
    whole_rows = lax.all_gather(frames, "tp", axis=1, tiled=True)
    normed = layer_norm(whole_rows, attn_gain)
    projected = jnp.einsum(
        "td,gdc->gtc", normed, query_key_value, preferred_element_type=jnp.float32
    ).astype(jnp.bfloat16)
    score_scale = 1.0 / math.sqrt(HEAD)
    query_heads = projected[0].reshape(frame_rows, heads_here, HEAD)
    initial = (
        jnp.full((heads_here, frame_rows), -1e30, jnp.float32),
        jnp.zeros((heads_here, frame_rows), jnp.float32),
        jnp.zeros((frame_rows, heads_here, HEAD), jnp.float32),
    )
    pieces = (
        lax.all_gather(projected[1], "ctx", axis=0, tiled=True),
        lax.all_gather(projected[2], "ctx", axis=0, tiled=True),
    )
    key_count = pieces[0].shape[0]
    block_len = 1024 if key_count > 1024 and key_count % 1024 == 0 else key_count
    key_blocks = pieces[0].reshape(key_count // block_len, block_len, heads_here, HEAD)
    value_blocks = pieces[1].reshape(key_count // block_len, block_len, heads_here, HEAD)

    def one_block(running, pieces_now):
        running_max, denominator, weighted = running
        key_block, value_block = pieces_now
        scores = (
            jnp.einsum("qhd,khd->hqk", query_heads, key_block, preferred_element_type=jnp.float32)
            * score_scale
        )
        new_max = jnp.maximum(running_max, jnp.max(scores, axis=-1))
        weights = jnp.exp(scores - new_max[:, :, None])
        rescale = jnp.exp(running_max - new_max)
        denominator = denominator * rescale + jnp.sum(weights, axis=-1)
        added = jnp.einsum(
            "hqk,khd->qhd",
            weights.astype(jnp.bfloat16),
            value_block,
            preferred_element_type=jnp.float32,
        )
        weighted = weighted * jnp.transpose(rescale)[:, :, None] + added
        return ((new_max, denominator, weighted), None)

    result, _ = lax.scan(one_block, initial, (key_blocks, value_blocks))
    running_max, denominator, weighted = result
    context = (
        (weighted / jnp.transpose(denominator)[:, :, None])
        .reshape(frame_rows, local_cols)
        .astype(jnp.bfloat16)
    )
    attn_terms = jnp.dot(context, out_weight, preferred_element_type=jnp.float32)
    summed = lax.psum(attn_terms.astype(jnp.bfloat16), "tp").astype(jnp.float32)
    middle_whole = (whole_rows.astype(jnp.float32) + summed).astype(jnp.bfloat16)
    middle = lax.dynamic_slice_in_dim(
        middle_whole, lax.axis_index("tp") * local_cols, local_cols, 1
    )
    normed_conv = layer_norm(middle_whole, conv_gain)
    halves = jnp.einsum("td,gdc->gtc", normed_conv, glu_weight, preferred_element_type=jnp.float32)
    glu = (halves[0] * jax.nn.sigmoid(halves[1])).astype(jnp.bfloat16)
    reach = depth_kernel.shape[0] // 2
    regrouped = lax.all_to_all(glu, "ctx", split_axis=1, concat_axis=0, tiled=True)
    group_cols = regrouped.shape[1]
    offset_cols = lax.axis_index("ctx") * group_cols
    kernel_part = lax.dynamic_slice_in_dim(depth_kernel, offset_cols, group_cols, 1)
    bias_part = lax.dynamic_slice_in_dim(depth_bias, offset_cols, group_cols, 0)
    padded = jnp.pad(regrouped, ((reach, reach), (0, 0)))
    activated_part = depthwise(padded, kernel_part, bias_part, regrouped.shape[0])
    activated = lax.all_to_all(activated_part, "ctx", split_axis=0, concat_axis=1, tiled=True)
    conv_terms = jnp.dot(activated, proj_weight, preferred_element_type=jnp.float32)
    conv_sum = lax.psum_scatter(
        conv_terms.astype(jnp.bfloat16), "tp", scatter_dimension=1, tiled=True
    ).astype(jnp.float32)
    return (middle.astype(jnp.float32) + conv_sum).astype(jnp.bfloat16)


def pick(table, row, column):
    value = 0
    for index, line in enumerate(table):
        value = value + jnp.where(row == index, line[column], 0)
    return value


def norm_rows(parts, gain, store):
    width = sum(part.shape[-1] for part in parts)
    total = sum(jnp.sum(part, axis=-1, keepdims=True) for part in parts)
    average = total / width
    centered = [part - average for part in parts]
    squares = sum(jnp.sum(part * part, axis=-1, keepdims=True) for part in centered)
    scale = lax.rsqrt(squares / width + 1e-05)
    start = 0
    for index, part in enumerate(centered):
        stop = start + part.shape[-1]
        store(index, (part * scale * gain[:, start:stop]).astype(jnp.bfloat16))
        start = stop


def fused_kernel(
    ctx_size,
    tp_size,
    frames,
    attn_gain,
    qkv,
    out_w,
    conv_gain,
    glu_w,
    depth_k,
    depth_b,
    proj_w,
    out,
    w_qkv,
    w_out,
    w_glu,
    w_proj,
    taps,
    taps32,
    attn_scale,
    conv_scale,
    bias,
    gathered,
    normed,
    q_all,
    k_all,
    v_all,
    context_out,
    context_in,
    part32,
    part16,
    pair_in,
    pair_sum,
    peer_in,
    middle,
    glu16,
    halo_low,
    halo_high,
    padded,
    act,
    conv32,
    conv16,
    conv_pair_in,
    conv_keep,
    conv_send,
    conv_peer_in,
    local_sem,
    gather_recv,
    sib_send,
    peer_send,
    up_send,
    down_send,
    ctx_send,
    ctx_recv,
    stage_send,
    stage_recv,
    halo_send,
    halo_recv,
):
    c = lax.axis_index("ctx")
    t = lax.axis_index("tp")
    y = t // 2
    k = t % 2
    sibling = y * 2 + (1 - k)
    peer = (1 - y) * 2 + k
    diagonal = (1 - y) * 2 + (1 - k)
    rows, cols = frames.shape
    step_rows = rows // ROW_CHUNKS

    def remote(source, target, send, receive, **device):
        return pltpu.make_async_remote_copy(
            src_ref=source,
            dst_ref=target,
            send_sem=send,
            recv_sem=receive,
            device_id=device,
            device_id_type=MESH,
        )

    first_col = c * HEAD
    window = jnp.minimum(first_col // 128, (cols - WINDOW) // 128)
    shift = first_col - window * 128
    window_cols = pl.ds(pl.multiple_of(window * 128, 128), WINDOW)

    part_rows = rows // PARTS

    def block(ctx_index, tp_index, part=None):
        if part is None:
            at = pl.ds(pl.multiple_of(ctx_index * rows, 16), rows)
        else:
            at = pl.ds(pl.multiple_of(ctx_index * rows + part * part_rows, 16), part_rows)
        return gathered.at[tp_index, at]

    local = [pltpu.make_async_copy(frames, block(c, t), local_sem.at[0])]
    for i in range(3):
        local.append(
            pltpu.make_async_copy(
                qkv.at[i, :, window_cols],
                w_qkv.at[:, pl.ds(i * WINDOW, WINDOW)],
                local_sem.at[1 + i],
            )
        )
    local.append(pltpu.make_async_copy(out_w, w_out, local_sem.at[4]))
    for i in range(2):
        local.append(
            pltpu.make_async_copy(
                glu_w.at[i], w_glu.at[:, pl.ds(i * cols, cols)], local_sem.at[5 + i]
            )
        )
    local.append(pltpu.make_async_copy(proj_w, w_proj, local_sem.at[7]))
    local.append(pltpu.make_async_copy(depth_k, taps, local_sem.at[8]))
    local.append(pltpu.make_async_copy(conv_gain, conv_scale, local_sem.at[9]))
    local.append(pltpu.make_async_copy(depth_b, bias, local_sem.at[10]))
    local.insert(4, pltpu.make_async_copy(attn_gain, attn_scale, local_sem.at[11]))

    barrier = pltpu.get_barrier_semaphore()
    for other in (sibling, peer):
        pl.semaphore_signal(barrier, inc=1, device_id={"tp": other}, device_id_type=MESH)
    for hop in range(1, ctx_size):
        pl.semaphore_signal(
            barrier, inc=1, device_id={"ctx": (c + hop) % ctx_size}, device_id_type=MESH
        )
    for copy in local:
        copy.start()
    pl.semaphore_wait(barrier, 2 + ctx_size - 1)

    def own_part(part):
        return frames.at[pl.ds(part * part_rows, part_rows)]

    def to_peer(index, part, source):
        return remote(
            source,
            block(index, t, part),
            peer_send.at[index, part],
            gather_recv.at[index, t, part],
            tp=peer,
        )

    def to_sibling(index, half, part, source):
        owner = half * 2 + k
        return remote(
            source,
            block(index, owner, part),
            sib_send.at[index, half, part],
            gather_recv.at[index, owner, part],
            tp=sibling,
        )

    def up(index, part, source):
        return remote(
            source,
            block(index, t, part),
            up_send.at[index, part],
            gather_recv.at[index, t, part],
            ctx=c + 1,
        )

    def down(index, part, source):
        return remote(
            source,
            block(index, t, part),
            down_send.at[index, part],
            gather_recv.at[index, t, part],
            ctx=c - 1,
        )

    def arrived(index, owner, part):
        here = block(index, owner, part)
        remote(
            here, here, peer_send.at[index, part], gather_recv.at[index, owner, part], tp=peer
        ).wait_recv()

    has_up = c + 1 < ctx_size
    has_down = c > 0

    for part in range(PARTS):
        source = own_part(part)
        pl.when(has_up)(lambda: up(c, part, source).start())
        pl.when(has_down)(lambda: down(c, part, source).start())
        to_peer(c, part, source).start()
        to_sibling(c, y, part, source).start()

    order = []
    for place in range(ctx_size):
        line = [place]
        for hop in range(1, ctx_size):
            line += [i for i in (place - hop, place + hop) if 0 <= i < ctx_size]
        order.append(line)

    key_lane = lax.broadcasted_iota(jnp.int32, (rows, WINDOW), 1)
    in_head = (key_lane >= shift) & (key_lane < shift + HEAD)
    select_row = lax.broadcasted_iota(jnp.int32, (WINDOW, 128), 0)
    select_col = lax.broadcasted_iota(jnp.int32, (WINDOW, 128), 1)
    select = ((select_row == select_col + shift) & (select_col < HEAD)).astype(jnp.bfloat16)

    def project(place):
        index = pick(order, c, place)
        start = pl.multiple_of(index * rows, 16)
        sub = part_rows // 2
        for part in range(PARTS):
            arrived(index, sibling, part)
            arrived(index, diagonal, part)
            for step in range(2 * part, 2 * part + 2):
                at = pl.ds(pl.multiple_of(start + step * sub, 16), sub)

                def store(piece, value):
                    normed[pl.ds(step * sub, sub), piece * cols : (piece + 1) * cols] = value

                norm_rows(
                    [gathered[i, at, :].astype(jnp.float32) for i in range(tp_size)],
                    attn_scale[...].reshape(1, -1),
                    store,
                )
        here = pl.ds(start, rows)
        projected = jnp.dot(normed[...], w_qkv[...], preferred_element_type=jnp.float32)
        q_all[here, :] = jnp.where(in_head, projected[:, :WINDOW], 0.0).astype(jnp.bfloat16)
        k_all[here, :] = projected[:, WINDOW : 2 * WINDOW].astype(jnp.bfloat16)
        v_all[here, :] = jnp.dot(
            projected[:, 2 * WINDOW :].astype(jnp.bfloat16),
            select,
            preferred_element_type=jnp.float32,
        ).astype(jnp.bfloat16)

    def pass_on(hop):
        for part in range(PARTS):

            @pl.when(c >= hop)
            def _():
                index = c - hop
                arrived(index, t, part)
                source = block(index, t, part)
                pl.when(has_up)(lambda: up(index, part, source).start())
                to_peer(index, part, source).start()
                to_sibling(index, y, part, source).start()

            @pl.when(c + hop < ctx_size)
            def _():
                index = c + hop
                arrived(index, t, part)
                source = block(index, t, part)
                pl.when(has_down)(lambda: down(index, part, source).start())
                to_peer(index, part, source).start()
                to_sibling(index, y, part, source).start()

    def from_peer(place):
        index = pick(order, c, place)
        for part in range(PARTS):
            arrived(index, peer, part)
            to_sibling(index, 1 - y, part, block(index, peer, part)).start()

    pass_on(1)
    from_peer(0)
    pass_on(2)
    from_peer(1)
    for i in range(5):
        local[i].wait()
    project(0)
    for place in range(2, ctx_size):
        last = place == ctx_size - 1
        if not last:
            pass_on(place + 1)
        else:
            project(place - 1)
        from_peer(place)
        if not last:
            project(place - 1)
    project(ctx_size - 1)

    score_scale = 1.0 / math.sqrt(HEAD)

    def chunk(step):
        return pl.ds(step * step_rows, step_rows)

    def context_copy(index, step):
        return remote(
            context_out.at[index, chunk(step)],
            context_in.at[c, chunk(step)],
            ctx_send.at[index, step],
            ctx_recv.at[c, step],
            ctx=index,
        )

    def attend(step, place):
        index = pick(order, c, place)
        here = pl.ds(pl.multiple_of(index * rows + step * step_rows, 16), step_rows)
        scores = (
            lax.dot_general(
                q_all[here, :],
                k_all[...],
                (((1,), (1,)), ((), ())),
                preferred_element_type=jnp.float32,
            )
            * score_scale
        )
        weights = jnp.exp(scores - jnp.max(scores, axis=-1, keepdims=True))
        denominator = jnp.sum(weights, axis=-1, keepdims=True)
        weighted = jnp.dot(
            weights.astype(jnp.bfloat16), v_all[...], preferred_element_type=jnp.float32
        )
        context = (weighted / denominator).astype(jnp.bfloat16)
        if place:
            context_out[index, chunk(step), :] = context
            context_copy(index, step).start()
        else:
            context_in[c, chunk(step), :] = context

    for step in range(ROW_CHUNKS):
        for place in reversed(range(ctx_size)):
            attend(step, place)
    local[5].wait()

    mine = pl.ds(2 * k, 2)
    others = pl.ds(2 * (1 - k), 2)

    def stage(kind, step, source, target, device):
        return remote(
            source, target, stage_send.at[kind, step], stage_recv.at[kind, step], tp=device
        )

    def pair_copy(step):
        return stage(0, step, part16.at[others, chunk(step)], pair_in.at[:, chunk(step)], sibling)

    def peer_copy(step):
        return stage(1, step, pair_sum.at[:, chunk(step)], peer_in.at[:, chunk(step)], peer)

    def middle_copy(step, half):
        ref = middle.at[half, chunk(step)]
        return stage(2, step, ref, ref, sibling)

    for step in range(ROW_CHUNKS):
        for hop in range(1, ctx_size):
            index = (c + hop) % ctx_size
            here = context_in.at[index, chunk(step)]
            remote(here, here, ctx_send.at[index, step], ctx_recv.at[index, step], ctx=index).wait_recv()
        terms = sum(
            jnp.dot(
                context_in[head, chunk(step), :HEAD],
                w_out[head * HEAD : (head + 1) * HEAD, :],
                preferred_element_type=jnp.float32,
            )
            for head in range(ctx_size)
        )
        for i in range(tp_size):
            piece = terms[:, i * cols : (i + 1) * cols]
            part32[i, chunk(step), :] = piece
            part16[i, chunk(step), :] = piece.astype(jnp.bfloat16)
        pair_copy(step).start()
    for step in range(ROW_CHUNKS):
        pair_copy(step).wait_recv()
        pair_sum[:, chunk(step), :] = (
            part32[mine, chunk(step), :] + pair_in[:, chunk(step), :].astype(jnp.float32)
        ).astype(jnp.bfloat16)
        peer_copy(step).start()

    for i in range(6, 12):
        local[i].wait()
    taps32[...] = taps[...].astype(jnp.float32)

    def halo_up():
        return remote(
            glu16.at[pl.ds(rows - HALO, HALO)], halo_low, halo_send.at[0], halo_recv.at[0], ctx=c + 1
        )

    def halo_down():
        return remote(glu16.at[pl.ds(0, HALO)], halo_high, halo_send.at[1], halo_recv.at[1], ctx=c - 1)

    for step in range(ROW_CHUNKS):
        peer_copy(step).wait_recv()
        own = pl.ds(pl.multiple_of(c * rows + step * step_rows, 16), step_rows)
        summed = pair_sum[:, chunk(step), :].astype(jnp.float32) + peer_in[
            :, chunk(step), :
        ].astype(jnp.float32)
        middle[mine, chunk(step), :] = (
            gathered[mine, own, :].astype(jnp.float32) + summed
        ).astype(jnp.bfloat16)
        middle_copy(step, mine).start()
        middle_copy(step, others).wait_recv()

        def store(part, value):
            normed[chunk(step), part * cols : (part + 1) * cols] = value

        norm_rows(
            [middle[i, chunk(step), :].astype(jnp.float32) for i in range(tp_size)],
            conv_scale[...].reshape(1, -1),
            store,
        )
        halves = jnp.dot(normed[chunk(step), :], w_glu[...], preferred_element_type=jnp.float32)
        glu = (halves[:, :cols] * jax.nn.sigmoid(halves[:, cols:])).astype(jnp.bfloat16)
        glu16[chunk(step), :] = glu
        padded[HALO + step * step_rows : HALO + (step + 1) * step_rows, :] = glu.astype(jnp.float32)
        if step == 0:
            pl.when(has_down)(lambda: halo_down().start())
        if step == ROW_CHUNKS - 1:
            pl.when(has_up)(lambda: halo_up().start())

    def edge_low():
        padded[0:HALO, :] = jnp.zeros((HALO, cols), jnp.float32)

        @pl.when(has_down)
        def _():
            halo_up().wait_recv()
            padded[0:HALO, :] = halo_low[...].astype(jnp.float32)

    def edge_high():
        padded[HALO + rows :, :] = jnp.zeros((HALO, cols), jnp.float32)

        @pl.when(has_up)
        def _():
            halo_down().wait_recv()
            padded[HALO + rows :, :] = halo_high[...].astype(jnp.float32)

    def conv_pair(step):
        return stage(
            3, step, conv16.at[others, chunk(step)], conv_pair_in.at[:, chunk(step)], sibling
        )

    def conv_peer(step):
        return stage(4, step, conv_send.at[chunk(step)], conv_peer_in.at[chunk(step)], peer)

    tap_count = taps32.shape[0]
    first = HALO - tap_count // 2
    last_first = list(reversed(range(ROW_CHUNKS)))
    for step in last_first:
        if step == ROW_CHUNKS - 1:
            edge_high()
        if step == 0:
            edge_low()
        for lane in range(0, cols, 128):
            lanes = slice(lane, lane + 128)
            total = jnp.zeros((step_rows, 128), jnp.float32)
            for tap in range(tap_count):
                at = step * step_rows + first + tap
                total = total + padded[at : at + step_rows, lanes] * taps32[tap : tap + 1, lanes]
            total = total + bias[lanes].reshape(1, -1)
            act[chunk(step), lanes] = (total / (1.0 + jnp.exp(-total))).astype(jnp.bfloat16)
        terms = jnp.dot(act[chunk(step), :], w_proj[...], preferred_element_type=jnp.float32)
        for i in range(tp_size):
            piece = terms[:, i * cols : (i + 1) * cols]
            slot = (i % 2) * 2 + i // 2
            conv32[slot, chunk(step), :] = piece
            conv16[slot, chunk(step), :] = piece.astype(jnp.bfloat16)
        conv_pair(step).start()
    for step in last_first:
        conv_pair(step).wait_recv()
        conv_send[chunk(step), :] = (
            conv32[2 * k + 1 - y, chunk(step), :]
            + conv_pair_in[1 - y, chunk(step), :].astype(jnp.float32)
        ).astype(jnp.bfloat16)
        conv_peer(step).start()
        conv_keep[chunk(step), :] = (
            conv32[2 * k + y, chunk(step), :]
            + conv_pair_in[y, chunk(step), :].astype(jnp.float32)
            + middle[t, chunk(step), :].astype(jnp.float32)
        )
    for step in last_first:
        conv_peer(step).wait_recv()
        out[chunk(step), :] = (
            conv_keep[chunk(step), :] + conv_peer_in[chunk(step), :].astype(jnp.float32)
        ).astype(jnp.bfloat16)

    for place in range(ctx_size):
        for part in range(PARTS):
            index = pick(order, c, place)
            source = block(index, t, part)
            pl.when(has_up & (index <= c))(lambda: up(index, part, source).wait_send())
            pl.when(has_down & (index >= c))(lambda: down(index, part, source).wait_send())
            to_peer(index, part, source).wait_send()
            to_sibling(index, y, part, source).wait_send()
            to_sibling(index, 1 - y, part, source).wait_send()
    for hop in range(1, ctx_size):
        for step in range(ROW_CHUNKS):
            context_copy((c + hop) % ctx_size, step).wait_send()
    for step in range(ROW_CHUNKS):
        pair_copy(step).wait_send()
        peer_copy(step).wait_send()
        middle_copy(step, mine).wait_send()
        conv_pair(step).wait_send()
        conv_peer(step).wait_send()
    pl.when(has_up)(lambda: halo_up().wait_send())
    pl.when(has_down)(lambda: halo_down().wait_send())


def fused(
    ctx_size,
    tp_size,
    frames,
    attn_gain,
    query_key_value,
    out_weight,
    conv_gain,
    glu_weight,
    depth_kernel,
    depth_bias,
    proj_weight,
):
    rows, cols = frames.shape
    width = cols * tp_size
    all_rows = rows * ctx_size
    taps = depth_kernel.shape[0]
    wide, narrow = jnp.float32, jnp.bfloat16
    vmem = pl.BlockSpec(memory_space=pltpu.VMEM)
    away = pl.BlockSpec(memory_space=pltpu.HBM)
    dma = pltpu.SemaphoreType.DMA
    return pl.pallas_call(
        functools.partial(fused_kernel, ctx_size, tp_size),
        out_shape=jax.ShapeDtypeStruct((rows, cols), narrow),
        in_specs=[away] * 9,
        out_specs=vmem,
        scratch_shapes=[
            pltpu.VMEM((width, 3 * WINDOW), narrow),
            pltpu.VMEM((cols, width), narrow),
            pltpu.VMEM((width, 2 * cols), narrow),
            pltpu.VMEM((cols, width), narrow),
            pltpu.VMEM((taps, cols), narrow),
            pltpu.VMEM((taps, cols), wide),
            pltpu.VMEM((width,), wide),
            pltpu.VMEM((width,), wide),
            pltpu.VMEM((cols,), wide),
            pltpu.VMEM((tp_size, all_rows, cols), narrow),
            pltpu.VMEM((rows, width), narrow),
            pltpu.VMEM((all_rows, WINDOW), narrow),
            pltpu.VMEM((all_rows, WINDOW), narrow),
            pltpu.VMEM((all_rows, 128), narrow),
            pltpu.VMEM((ctx_size, rows, 128), narrow),
            pltpu.VMEM((ctx_size, rows, 128), narrow),
            pltpu.VMEM((tp_size, rows, cols), wide),
            pltpu.VMEM((tp_size, rows, cols), narrow),
            pltpu.VMEM((2, rows, cols), narrow),
            pltpu.VMEM((2, rows, cols), narrow),
            pltpu.VMEM((2, rows, cols), narrow),
            pltpu.VMEM((tp_size, rows, cols), narrow),
            pltpu.VMEM((rows, cols), narrow),
            pltpu.VMEM((HALO, cols), narrow),
            pltpu.VMEM((HALO, cols), narrow),
            pltpu.VMEM((rows + 2 * HALO, cols), wide),
            pltpu.VMEM((rows, cols), narrow),
            pltpu.VMEM((tp_size, rows, cols), wide),
            pltpu.VMEM((tp_size, rows, cols), narrow),
            pltpu.VMEM((2, rows, cols), narrow),
            pltpu.VMEM((rows, cols), wide),
            pltpu.VMEM((rows, cols), narrow),
            pltpu.VMEM((rows, cols), narrow),
            dma((12,)),
            dma((ctx_size, tp_size, PARTS)),
            dma((ctx_size, 2, PARTS)),
            dma((ctx_size, PARTS)),
            dma((ctx_size, PARTS)),
            dma((ctx_size, PARTS)),
            dma((ctx_size, ROW_CHUNKS)),
            dma((ctx_size, ROW_CHUNKS)),
            dma((5, ROW_CHUNKS)),
            dma((5, ROW_CHUNKS)),
            dma((2,)),
            dma((2,)),
        ],
        compiler_params=pltpu.CompilerParams(
            collective_id=0, has_side_effects=True, vmem_limit_bytes=62 * 1024 * 1024
        ),
    )(
        frames,
        attn_gain,
        query_key_value,
        out_weight,
        conv_gain,
        glu_weight,
        depth_kernel,
        depth_bias,
        proj_weight,
    )


def solution(mesh):
    in_specs = (
        P(("batch", "ctx"), "tp"),
        P(),
        P(None, None, "tp"),
        P("tp", None),
        P(),
        P(None, None, "tp"),
        P(None, "tp"),
        P("tp"),
        P("tp", None),
    )
    out_specs = P(("batch", "ctx"), "tp")
    ctx_size, tp_size = mesh.shape["ctx"], mesh.shape["tp"]

    def body(frames, attn_gain, query_key_value, *rest):
        one_head_each = ctx_size * HEAD == query_key_value.shape[2]
        even = frames.shape[0] % (16 * ROW_CHUNKS * PARTS) == 0
        if tp_size == 4 and one_head_each and ctx_size > 2 and even:
            return fused(ctx_size, tp_size, frames, attn_gain, query_key_value, *rest)
        return per_device(frames, attn_gain, query_key_value, *rest)

    return jax.shard_map(
        body, mesh=mesh, in_specs=in_specs, out_specs=out_specs, check_vma=False
    )
```

```python
import functools
import math

import jax
import jax.numpy as jnp
from jax import lax
from jax.experimental import pallas as pl
from jax.experimental.pallas import tpu as pltpu
from jax.sharding import PartitionSpec as P

HEAD = 96
HALO = 16
ROW_CHUNKS = 2
PARTS = 2
WINDOW = 256
MESH = pl.DeviceIdType.MESH


def layer_norm(inputs, gain):
    inputs = inputs.astype(jnp.float32)
    average = jnp.mean(inputs, axis=-1, keepdims=True)
    centered = inputs - average
    variance = jnp.mean(centered * centered, axis=-1, keepdims=True)
    return (centered * lax.rsqrt(variance + 1e-05) * gain).astype(jnp.bfloat16)


def depthwise(padded, kernel, bias, count):
    convolved = jnp.zeros((count, padded.shape[1]), jnp.float32)
    for kernel_tap in range(kernel.shape[0]):
        convolved = convolved + padded[kernel_tap : kernel_tap + count].astype(
            jnp.float32
        ) * kernel[kernel_tap].astype(jnp.float32)
    return jax.nn.silu(convolved + bias).astype(jnp.bfloat16)


def per_device(
    frames,
    attn_gain,
    query_key_value,
    out_weight,
    conv_gain,
    glu_weight,
    depth_kernel,
    depth_bias,
    proj_weight,
):
    frame_rows = frames.shape[0]
    local_cols = frames.shape[1]
    heads_here = query_key_value.shape[2] // HEAD
    whole_rows = lax.all_gather(frames, "tp", axis=1, tiled=True)
    normed = layer_norm(whole_rows, attn_gain)
    projected = jnp.einsum(
        "td,gdc->gtc", normed, query_key_value, preferred_element_type=jnp.float32
    ).astype(jnp.bfloat16)
    score_scale = 1.0 / math.sqrt(HEAD)
    query_heads = projected[0].reshape(frame_rows, heads_here, HEAD)
    initial = (
        jnp.full((heads_here, frame_rows), -1e30, jnp.float32),
        jnp.zeros((heads_here, frame_rows), jnp.float32),
        jnp.zeros((frame_rows, heads_here, HEAD), jnp.float32),
    )
    pieces = (
        lax.all_gather(projected[1], "ctx", axis=0, tiled=True),
        lax.all_gather(projected[2], "ctx", axis=0, tiled=True),
    )
    key_count = pieces[0].shape[0]
    block_len = 1024 if key_count > 1024 and key_count % 1024 == 0 else key_count
    key_blocks = pieces[0].reshape(key_count // block_len, block_len, heads_here, HEAD)
    value_blocks = pieces[1].reshape(key_count // block_len, block_len, heads_here, HEAD)

    def one_block(running, pieces_now):
        running_max, denominator, weighted = running
        key_block, value_block = pieces_now
        scores = (
            jnp.einsum("qhd,khd->hqk", query_heads, key_block, preferred_element_type=jnp.float32)
            * score_scale
        )
        new_max = jnp.maximum(running_max, jnp.max(scores, axis=-1))
        weights = jnp.exp(scores - new_max[:, :, None])
        rescale = jnp.exp(running_max - new_max)
        denominator = denominator * rescale + jnp.sum(weights, axis=-1)
        added = jnp.einsum(
            "hqk,khd->qhd",
            weights.astype(jnp.bfloat16),
            value_block,
            preferred_element_type=jnp.float32,
        )
        weighted = weighted * jnp.transpose(rescale)[:, :, None] + added
        return ((new_max, denominator, weighted), None)

    result, _ = lax.scan(one_block, initial, (key_blocks, value_blocks))
    running_max, denominator, weighted = result
    context = (
        (weighted / jnp.transpose(denominator)[:, :, None])
        .reshape(frame_rows, local_cols)
        .astype(jnp.bfloat16)
    )
    attn_terms = jnp.dot(context, out_weight, preferred_element_type=jnp.float32)
    summed = lax.psum(attn_terms.astype(jnp.bfloat16), "tp").astype(jnp.float32)
    middle_whole = (whole_rows.astype(jnp.float32) + summed).astype(jnp.bfloat16)
    middle = lax.dynamic_slice_in_dim(
        middle_whole, lax.axis_index("tp") * local_cols, local_cols, 1
    )
    normed_conv = layer_norm(middle_whole, conv_gain)
    halves = jnp.einsum("td,gdc->gtc", normed_conv, glu_weight, preferred_element_type=jnp.float32)
    glu = (halves[0] * jax.nn.sigmoid(halves[1])).astype(jnp.bfloat16)
    reach = depth_kernel.shape[0] // 2
    regrouped = lax.all_to_all(glu, "ctx", split_axis=1, concat_axis=0, tiled=True)
    group_cols = regrouped.shape[1]
    offset_cols = lax.axis_index("ctx") * group_cols
    kernel_part = lax.dynamic_slice_in_dim(depth_kernel, offset_cols, group_cols, 1)
    bias_part = lax.dynamic_slice_in_dim(depth_bias, offset_cols, group_cols, 0)
    padded = jnp.pad(regrouped, ((reach, reach), (0, 0)))
    activated_part = depthwise(padded, kernel_part, bias_part, regrouped.shape[0])
    activated = lax.all_to_all(activated_part, "ctx", split_axis=0, concat_axis=1, tiled=True)
    conv_terms = jnp.dot(activated, proj_weight, preferred_element_type=jnp.float32)
    conv_sum = lax.psum_scatter(
        conv_terms.astype(jnp.bfloat16), "tp", scatter_dimension=1, tiled=True
    ).astype(jnp.float32)
    return (middle.astype(jnp.float32) + conv_sum).astype(jnp.bfloat16)


def pick(table, row, column):
    value = 0
    for index, line in enumerate(table):
        value = value + jnp.where(row == index, line[column], 0)
    return value


def norm_rows(parts, gain, store):
    width = sum(part.shape[-1] for part in parts)
    total = sum(jnp.sum(part, axis=-1, keepdims=True) for part in parts)
    average = total / width
    centered = [part - average for part in parts]
    squares = sum(jnp.sum(part * part, axis=-1, keepdims=True) for part in centered)
    scale = lax.rsqrt(squares / width + 1e-05)
    start = 0
    for index, part in enumerate(centered):
        stop = start + part.shape[-1]
        store(index, (part * scale * gain[:, start:stop]).astype(jnp.bfloat16))
        start = stop


def fused_kernel(
    ctx_size,
    tp_size,
    frames,
    attn_gain,
    qkv,
    out_w,
    conv_gain,
    glu_w,
    depth_k,
    depth_b,
    proj_w,
    out,
    w_qkv,
    w_out,
    w_glu,
    w_proj,
    taps,
    taps32,
    attn_scale,
    conv_scale,
    bias,
    gathered,
    normed,
    q_all,
    k_all,
    v_all,
    context_out,
    context_in,
    part32,
    part16,
    pair_in,
    pair_sum,
    peer_in,
    middle,
    glu16,
    halo_low,
    halo_high,
    padded,
    act,
    conv32,
    conv16,
    conv_pair_in,
    conv_keep,
    conv_send,
    conv_peer_in,
    local_sem,
    gather_recv,
    sib_send,
    peer_send,
    up_send,
    down_send,
    side_send,
    ctx_send,
    ctx_recv,
    stage_send,
    stage_recv,
    halo_send,
    halo_recv,
):
    c = lax.axis_index("ctx")
    t = lax.axis_index("tp")
    y = t // 2
    k = t % 2
    sibling = y * 2 + (1 - k)
    peer = (1 - y) * 2 + k
    diagonal = (1 - y) * 2 + (1 - k)
    rows, cols = frames.shape
    step_rows = rows // ROW_CHUNKS

    def remote(source, target, send, receive, **device):
        return pltpu.make_async_remote_copy(
            src_ref=source,
            dst_ref=target,
            send_sem=send,
            recv_sem=receive,
            device_id=device,
            device_id_type=MESH,
        )

    first_col = c * HEAD
    window = jnp.minimum(first_col // 128, (cols - WINDOW) // 128)
    shift = first_col - window * 128
    window_cols = pl.ds(pl.multiple_of(window * 128, 128), WINDOW)

    part_rows = rows // PARTS

    def block(ctx_index, tp_index, part=None):
        if part is None:
            at = pl.ds(pl.multiple_of(ctx_index * rows, 16), rows)
        else:
            at = pl.ds(pl.multiple_of(ctx_index * rows + part * part_rows, 16), part_rows)
        return gathered.at[tp_index, at]

    local = [pltpu.make_async_copy(frames, block(c, t), local_sem.at[0])]
    for i in range(3):
        local.append(
            pltpu.make_async_copy(
                qkv.at[i, :, window_cols],
                w_qkv.at[:, pl.ds(i * WINDOW, WINDOW)],
                local_sem.at[1 + i],
            )
        )
    local.append(pltpu.make_async_copy(out_w, w_out, local_sem.at[4]))
    for i in range(2):
        local.append(
            pltpu.make_async_copy(
                glu_w.at[i], w_glu.at[:, pl.ds(i * cols, cols)], local_sem.at[5 + i]
            )
        )
    local.append(pltpu.make_async_copy(proj_w, w_proj, local_sem.at[7]))
    local.append(pltpu.make_async_copy(depth_k, taps, local_sem.at[8]))
    local.append(pltpu.make_async_copy(conv_gain, conv_scale, local_sem.at[9]))
    local.append(pltpu.make_async_copy(depth_b, bias, local_sem.at[10]))
    local.insert(4, pltpu.make_async_copy(attn_gain, attn_scale, local_sem.at[11]))

    barrier = pltpu.get_barrier_semaphore()
    for other in (sibling, peer):
        pl.semaphore_signal(barrier, inc=1, device_id={"tp": other}, device_id_type=MESH)
    for hop in range(1, ctx_size):
        pl.semaphore_signal(
            barrier, inc=1, device_id={"ctx": (c + hop) % ctx_size}, device_id_type=MESH
        )
    for copy in local:
        copy.start()
    pl.semaphore_wait(barrier, 2 + ctx_size - 1)

    def own_part(part):
        return frames.at[pl.ds(part * part_rows, part_rows)]

    def to_peer(index, part, source):
        return remote(
            source,
            block(index, t, part),
            peer_send.at[index, part],
            gather_recv.at[index, t, part],
            tp=peer,
        )

    def to_sibling(index, half, part, source):
        owner = half * 2 + k
        return remote(
            source,
            block(index, owner, part),
            sib_send.at[index, half, part],
            gather_recv.at[index, owner, part],
            tp=sibling,
        )

    def up(index, part, source):
        return remote(
            source,
            block(index, t, part),
            up_send.at[index, part],
            gather_recv.at[index, t, part],
            ctx=c + 1,
        )

    def down(index, part, source):
        return remote(
            source,
            block(index, t, part),
            down_send.at[index, part],
            gather_recv.at[index, t, part],
            ctx=c - 1,
        )

    end = ctx_size - 1
    late = PARTS - 1

    def side_up():
        here = block(0, peer, late)
        return remote(here, here, side_send.at[0], gather_recv.at[0, peer, late], ctx=c + 1)

    def side_down():
        here = block(end, peer, late)
        return remote(here, here, side_send.at[1], gather_recv.at[end, peer, late], ctx=c - 1)

    def arrived(index, owner, part):
        here = block(index, owner, part)
        remote(
            here, here, peer_send.at[index, part], gather_recv.at[index, owner, part], tp=peer
        ).wait_recv()

    has_up = c + 1 < ctx_size
    has_down = c > 0

    for part in range(PARTS):
        source = own_part(part)
        pl.when(has_up)(lambda: up(c, part, source).start())
        pl.when(has_down)(lambda: down(c, part, source).start())
        to_peer(c, part, source).start()
        to_sibling(c, y, part, source).start()

    order = []
    for place in range(ctx_size):
        line = [place]
        for hop in range(1, ctx_size):
            line += [i for i in (place - hop, place + hop) if 0 <= i < ctx_size]
        order.append(line)

    key_lane = lax.broadcasted_iota(jnp.int32, (rows, WINDOW), 1)
    in_head = (key_lane >= shift) & (key_lane < shift + HEAD)
    select_row = lax.broadcasted_iota(jnp.int32, (WINDOW, 128), 0)
    select_col = lax.broadcasted_iota(jnp.int32, (WINDOW, 128), 1)
    select = ((select_row == select_col + shift) & (select_col < HEAD)).astype(jnp.bfloat16)

    def project(place):
        index = pick(order, c, place)
        start = pl.multiple_of(index * rows, 16)
        sub = part_rows // 2
        for part in range(PARTS):
            arrived(index, sibling, part)
            arrived(index, diagonal, part)
            for step in range(2 * part, 2 * part + 2):
                at = pl.ds(pl.multiple_of(start + step * sub, 16), sub)

                def store(piece, value):
                    normed[pl.ds(step * sub, sub), piece * cols : (piece + 1) * cols] = value

                norm_rows(
                    [gathered[i, at, :].astype(jnp.float32) for i in range(tp_size)],
                    attn_scale[...].reshape(1, -1),
                    store,
                )
        here = pl.ds(start, rows)
        projected = jnp.dot(normed[...], w_qkv[...], preferred_element_type=jnp.float32)
        q_all[here, :] = jnp.where(in_head, projected[:, :WINDOW], 0.0).astype(jnp.bfloat16)
        k_all[here, :] = projected[:, WINDOW : 2 * WINDOW].astype(jnp.bfloat16)
        v_all[here, :] = jnp.dot(
            projected[:, 2 * WINDOW :].astype(jnp.bfloat16),
            select,
            preferred_element_type=jnp.float32,
        ).astype(jnp.bfloat16)

    def pass_on(hop):
        for part in range(PARTS):

            @pl.when(c >= hop)
            def _():
                index = c - hop
                arrived(index, t, part)
                source = block(index, t, part)
                pl.when(has_up)(lambda: up(index, part, source).start())
                if part == late:
                    pl.when(index > 0)(lambda: to_peer(index, part, source).start())
                else:
                    to_peer(index, part, source).start()
                to_sibling(index, y, part, source).start()

            @pl.when(c + hop < ctx_size)
            def _():
                index = c + hop
                arrived(index, t, part)
                source = block(index, t, part)
                pl.when(has_down)(lambda: down(index, part, source).start())
                if part == late:
                    pl.when(index < end)(lambda: to_peer(index, part, source).start())
                else:
                    to_peer(index, part, source).start()
                to_sibling(index, y, part, source).start()

    def pass_side(hop):
        @pl.when(c == hop)
        def _():
            arrived(0, peer, late)
            pl.when(has_up)(lambda: side_up().start())
            to_sibling(0, 1 - y, late, block(0, peer, late)).start()

        @pl.when(c + hop == end)
        def _():
            arrived(end, peer, late)
            pl.when(has_down)(lambda: side_down().start())
            to_sibling(end, 1 - y, late, block(end, peer, late)).start()

    def from_peer(place):
        index = pick(order, c, place)

        def take(part):
            arrived(index, peer, part)
            to_sibling(index, 1 - y, part, block(index, peer, part)).start()

        for part in range(PARTS):
            if part == late and place:
                pl.when((index > 0) & (index < end))(lambda: take(part))
            else:
                take(part)
        if not place:
            pl.when(c == 0)(lambda: side_up().start())
            pl.when(c == end)(lambda: side_down().start())

    pass_on(1)
    from_peer(0)
    pass_on(2)
    pass_side(1)
    from_peer(1)
    for i in range(5):
        local[i].wait()
    project(0)
    for place in range(2, ctx_size):
        last = place == ctx_size - 1
        if not last:
            pass_on(place + 1)
        else:
            project(place - 1)
        pass_side(place)
        from_peer(place)
        if not last:
            project(place - 1)
    project(ctx_size - 1)

    score_scale = 1.0 / math.sqrt(HEAD)

    def chunk(step):
        return pl.ds(step * step_rows, step_rows)

    def context_copy(index, step):
        return remote(
            context_out.at[index, chunk(step)],
            context_in.at[c, chunk(step)],
            ctx_send.at[index, step],
            ctx_recv.at[c, step],
            ctx=index,
        )

    def attend(step, place):
        index = pick(order, c, place)
        here = pl.ds(pl.multiple_of(index * rows + step * step_rows, 16), step_rows)
        scores = (
            lax.dot_general(
                q_all[here, :],
                k_all[...],
                (((1,), (1,)), ((), ())),
                preferred_element_type=jnp.float32,
            )
            * score_scale
        )
        weights = jnp.exp(scores - jnp.max(scores, axis=-1, keepdims=True))
        denominator = jnp.sum(weights, axis=-1, keepdims=True)
        weighted = jnp.dot(
            weights.astype(jnp.bfloat16), v_all[...], preferred_element_type=jnp.float32
        )
        context = (weighted / denominator).astype(jnp.bfloat16)
        if place:
            context_out[index, chunk(step), :] = context
            context_copy(index, step).start()
        else:
            context_in[c, chunk(step), :] = context

    for step in range(ROW_CHUNKS):
        for place in reversed(range(ctx_size)):
            attend(step, place)
    local[5].wait()

    mine = pl.ds(2 * k, 2)
    others = pl.ds(2 * (1 - k), 2)

    def stage(kind, step, source, target, device):
        return remote(
            source, target, stage_send.at[kind, step], stage_recv.at[kind, step], tp=device
        )

    def pair_copy(step):
        return stage(0, step, part16.at[others, chunk(step)], pair_in.at[:, chunk(step)], sibling)

    def peer_copy(step):
        return stage(1, step, pair_sum.at[:, chunk(step)], peer_in.at[:, chunk(step)], peer)

    def middle_copy(step, half):
        ref = middle.at[half, chunk(step)]
        return stage(2, step, ref, ref, sibling)

    for step in range(ROW_CHUNKS):
        for hop in range(1, ctx_size):
            index = (c + hop) % ctx_size
            here = context_in.at[index, chunk(step)]
            remote(here, here, ctx_send.at[index, step], ctx_recv.at[index, step], ctx=index).wait_recv()
        terms = sum(
            jnp.dot(
                context_in[head, chunk(step), :HEAD],
                w_out[head * HEAD : (head + 1) * HEAD, :],
                preferred_element_type=jnp.float32,
            )
            for head in range(ctx_size)
        )
        for i in range(tp_size):
            piece = terms[:, i * cols : (i + 1) * cols]
            part32[i, chunk(step), :] = piece
            part16[i, chunk(step), :] = piece.astype(jnp.bfloat16)
        pair_copy(step).start()
    for step in range(ROW_CHUNKS):
        pair_copy(step).wait_recv()
        pair_sum[:, chunk(step), :] = (
            part32[mine, chunk(step), :] + pair_in[:, chunk(step), :].astype(jnp.float32)
        ).astype(jnp.bfloat16)
        peer_copy(step).start()

    for i in range(6, 12):
        local[i].wait()
    taps32[...] = taps[...].astype(jnp.float32)

    def halo_up():
        return remote(
            glu16.at[pl.ds(rows - HALO, HALO)], halo_low, halo_send.at[0], halo_recv.at[0], ctx=c + 1
        )

    def halo_down():
        return remote(glu16.at[pl.ds(0, HALO)], halo_high, halo_send.at[1], halo_recv.at[1], ctx=c - 1)

    for step in range(ROW_CHUNKS):
        peer_copy(step).wait_recv()
        own = pl.ds(pl.multiple_of(c * rows + step * step_rows, 16), step_rows)
        summed = pair_sum[:, chunk(step), :].astype(jnp.float32) + peer_in[
            :, chunk(step), :
        ].astype(jnp.float32)
        middle[mine, chunk(step), :] = (
            gathered[mine, own, :].astype(jnp.float32) + summed
        ).astype(jnp.bfloat16)
        middle_copy(step, mine).start()
        middle_copy(step, others).wait_recv()

        def store(part, value):
            normed[chunk(step), part * cols : (part + 1) * cols] = value

        norm_rows(
            [middle[i, chunk(step), :].astype(jnp.float32) for i in range(tp_size)],
            conv_scale[...].reshape(1, -1),
            store,
        )
        halves = jnp.dot(normed[chunk(step), :], w_glu[...], preferred_element_type=jnp.float32)
        glu = (halves[:, :cols] * jax.nn.sigmoid(halves[:, cols:])).astype(jnp.bfloat16)
        glu16[chunk(step), :] = glu
        padded[HALO + step * step_rows : HALO + (step + 1) * step_rows, :] = glu.astype(jnp.float32)
        if step == 0:
            pl.when(has_down)(lambda: halo_down().start())
        if step == ROW_CHUNKS - 1:
            pl.when(has_up)(lambda: halo_up().start())

    def edge_low():
        padded[0:HALO, :] = jnp.zeros((HALO, cols), jnp.float32)

        @pl.when(has_down)
        def _():
            halo_up().wait_recv()
            padded[0:HALO, :] = halo_low[...].astype(jnp.float32)

    def edge_high():
        padded[HALO + rows :, :] = jnp.zeros((HALO, cols), jnp.float32)

        @pl.when(has_up)
        def _():
            halo_down().wait_recv()
            padded[HALO + rows :, :] = halo_high[...].astype(jnp.float32)

    def conv_pair(step):
        return stage(
            3, step, conv16.at[others, chunk(step)], conv_pair_in.at[:, chunk(step)], sibling
        )

    def conv_peer(step):
        return stage(4, step, conv_send.at[chunk(step)], conv_peer_in.at[chunk(step)], peer)

    tap_count = taps32.shape[0]
    first = HALO - tap_count // 2
    last_first = list(reversed(range(ROW_CHUNKS)))
    for step in last_first:
        if step == ROW_CHUNKS - 1:
            edge_high()
        if step == 0:
            edge_low()
        for lane in range(0, cols, 128):
            lanes = slice(lane, lane + 128)
            total = jnp.zeros((step_rows, 128), jnp.float32)
            for tap in range(tap_count):
                at = step * step_rows + first + tap
                total = total + padded[at : at + step_rows, lanes] * taps32[tap : tap + 1, lanes]
            total = total + bias[lanes].reshape(1, -1)
            act[chunk(step), lanes] = (total / (1.0 + jnp.exp(-total))).astype(jnp.bfloat16)
        terms = jnp.dot(act[chunk(step), :], w_proj[...], preferred_element_type=jnp.float32)
        for i in range(tp_size):
            piece = terms[:, i * cols : (i + 1) * cols]
            slot = (i % 2) * 2 + i // 2
            conv32[slot, chunk(step), :] = piece
            conv16[slot, chunk(step), :] = piece.astype(jnp.bfloat16)
        conv_pair(step).start()
    for step in last_first:
        conv_pair(step).wait_recv()
        conv_send[chunk(step), :] = (
            conv32[2 * k + 1 - y, chunk(step), :]
            + conv_pair_in[1 - y, chunk(step), :].astype(jnp.float32)
        ).astype(jnp.bfloat16)
        conv_peer(step).start()
        conv_keep[chunk(step), :] = (
            conv32[2 * k + y, chunk(step), :]
            + conv_pair_in[y, chunk(step), :].astype(jnp.float32)
            + middle[t, chunk(step), :].astype(jnp.float32)
        )
    for step in last_first:
        conv_peer(step).wait_recv()
        out[chunk(step), :] = (
            conv_keep[chunk(step), :] + conv_peer_in[chunk(step), :].astype(jnp.float32)
        ).astype(jnp.bfloat16)

    for place in range(ctx_size):
        for part in range(PARTS):
            index = pick(order, c, place)
            source = block(index, t, part)
            pl.when(has_up & (index <= c))(lambda: up(index, part, source).wait_send())
            pl.when(has_down & (index >= c))(lambda: down(index, part, source).wait_send())
            if part == late:
                crossed = (index == c) | ((index > 0) & (index < end))
                pl.when(crossed)(lambda: to_peer(index, part, source).wait_send())
            else:
                to_peer(index, part, source).wait_send()
            to_sibling(index, y, part, source).wait_send()
            to_sibling(index, 1 - y, part, source).wait_send()
    pl.when(has_up)(lambda: side_up().wait_send())
    pl.when(has_down)(lambda: side_down().wait_send())
    for hop in range(1, ctx_size):
        for step in range(ROW_CHUNKS):
            context_copy((c + hop) % ctx_size, step).wait_send()
    for step in range(ROW_CHUNKS):
        pair_copy(step).wait_send()
        peer_copy(step).wait_send()
        middle_copy(step, mine).wait_send()
        conv_pair(step).wait_send()
        conv_peer(step).wait_send()
    pl.when(has_up)(lambda: halo_up().wait_send())
    pl.when(has_down)(lambda: halo_down().wait_send())


def fused(
    ctx_size,
    tp_size,
    frames,
    attn_gain,
    query_key_value,
    out_weight,
    conv_gain,
    glu_weight,
    depth_kernel,
    depth_bias,
    proj_weight,
):
    rows, cols = frames.shape
    width = cols * tp_size
    all_rows = rows * ctx_size
    taps = depth_kernel.shape[0]
    wide, narrow = jnp.float32, jnp.bfloat16
    vmem = pl.BlockSpec(memory_space=pltpu.VMEM)
    away = pl.BlockSpec(memory_space=pltpu.HBM)
    dma = pltpu.SemaphoreType.DMA
    return pl.pallas_call(
        functools.partial(fused_kernel, ctx_size, tp_size),
        out_shape=jax.ShapeDtypeStruct((rows, cols), narrow),
        in_specs=[away] * 9,
        out_specs=vmem,
        scratch_shapes=[
            pltpu.VMEM((width, 3 * WINDOW), narrow),
            pltpu.VMEM((cols, width), narrow),
            pltpu.VMEM((width, 2 * cols), narrow),
            pltpu.VMEM((cols, width), narrow),
            pltpu.VMEM((taps, cols), narrow),
            pltpu.VMEM((taps, cols), wide),
            pltpu.VMEM((width,), wide),
            pltpu.VMEM((width,), wide),
            pltpu.VMEM((cols,), wide),
            pltpu.VMEM((tp_size, all_rows, cols), narrow),
            pltpu.VMEM((rows, width), narrow),
            pltpu.VMEM((all_rows, WINDOW), narrow),
            pltpu.VMEM((all_rows, WINDOW), narrow),
            pltpu.VMEM((all_rows, 128), narrow),
            pltpu.VMEM((ctx_size, rows, 128), narrow),
            pltpu.VMEM((ctx_size, rows, 128), narrow),
            pltpu.VMEM((tp_size, rows, cols), wide),
            pltpu.VMEM((tp_size, rows, cols), narrow),
            pltpu.VMEM((2, rows, cols), narrow),
            pltpu.VMEM((2, rows, cols), narrow),
            pltpu.VMEM((2, rows, cols), narrow),
            pltpu.VMEM((tp_size, rows, cols), narrow),
            pltpu.VMEM((rows, cols), narrow),
            pltpu.VMEM((HALO, cols), narrow),
            pltpu.VMEM((HALO, cols), narrow),
            pltpu.VMEM((rows + 2 * HALO, cols), wide),
            pltpu.VMEM((rows, cols), narrow),
            pltpu.VMEM((tp_size, rows, cols), wide),
            pltpu.VMEM((tp_size, rows, cols), narrow),
            pltpu.VMEM((2, rows, cols), narrow),
            pltpu.VMEM((rows, cols), wide),
            pltpu.VMEM((rows, cols), narrow),
            pltpu.VMEM((rows, cols), narrow),
            dma((12,)),
            dma((ctx_size, tp_size, PARTS)),
            dma((ctx_size, 2, PARTS)),
            dma((ctx_size, PARTS)),
            dma((ctx_size, PARTS)),
            dma((ctx_size, PARTS)),
            dma((2,)),
            dma((ctx_size, ROW_CHUNKS)),
            dma((ctx_size, ROW_CHUNKS)),
            dma((5, ROW_CHUNKS)),
            dma((5, ROW_CHUNKS)),
            dma((2,)),
            dma((2,)),
        ],
        compiler_params=pltpu.CompilerParams(
            collective_id=0, has_side_effects=True, vmem_limit_bytes=62 * 1024 * 1024
        ),
    )(
        frames,
        attn_gain,
        query_key_value,
        out_weight,
        conv_gain,
        glu_weight,
        depth_kernel,
        depth_bias,
        proj_weight,
    )


def solution(mesh):
    in_specs = (
        P(("batch", "ctx"), "tp"),
        P(),
        P(None, None, "tp"),
        P("tp", None),
        P(),
        P(None, None, "tp"),
        P(None, "tp"),
        P("tp"),
        P("tp", None),
    )
    out_specs = P(("batch", "ctx"), "tp")
    ctx_size, tp_size = mesh.shape["ctx"], mesh.shape["tp"]

    def body(frames, attn_gain, query_key_value, *rest):
        one_head_each = ctx_size * HEAD == query_key_value.shape[2]
        even = frames.shape[0] % (16 * ROW_CHUNKS * PARTS) == 0
        if tp_size == 4 and one_head_each and ctx_size > 2 and even:
            return fused(ctx_size, tp_size, frames, attn_gain, query_key_value, *rest)
        return per_device(frames, attn_gain, query_key_value, *rest)

    return jax.shard_map(
        body, mesh=mesh, in_specs=in_specs, out_specs=out_specs, check_vma=False
    )
```

```python
import functools
import math

import jax
import jax.numpy as jnp
from jax import lax
from jax.experimental import pallas as pl
from jax.experimental.pallas import tpu as pltpu
from jax.sharding import PartitionSpec as P

HEAD = 96
HALO = 16
ROW_CHUNKS = 2
PARTS = 2
WINDOW = 256
SLOT = 128
MESH = pl.DeviceIdType.MESH


def layer_norm(inputs, gain):
    inputs = inputs.astype(jnp.float32)
    average = jnp.mean(inputs, axis=-1, keepdims=True)
    centered = inputs - average
    variance = jnp.mean(centered * centered, axis=-1, keepdims=True)
    return (centered * lax.rsqrt(variance + 1e-05) * gain).astype(jnp.bfloat16)


def depthwise(padded, kernel, bias, count):
    convolved = jnp.zeros((count, padded.shape[1]), jnp.float32)
    for kernel_tap in range(kernel.shape[0]):
        convolved = convolved + padded[kernel_tap : kernel_tap + count].astype(
            jnp.float32
        ) * kernel[kernel_tap].astype(jnp.float32)
    return jax.nn.silu(convolved + bias).astype(jnp.bfloat16)


def per_device(
    frames,
    attn_gain,
    query_key_value,
    out_weight,
    conv_gain,
    glu_weight,
    depth_kernel,
    depth_bias,
    proj_weight,
):
    frame_rows = frames.shape[0]
    local_cols = frames.shape[1]
    heads_here = query_key_value.shape[2] // HEAD
    whole_rows = lax.all_gather(frames, "tp", axis=1, tiled=True)
    normed = layer_norm(whole_rows, attn_gain)
    projected = jnp.einsum(
        "td,gdc->gtc", normed, query_key_value, preferred_element_type=jnp.float32
    ).astype(jnp.bfloat16)
    score_scale = 1.0 / math.sqrt(HEAD)
    query_heads = projected[0].reshape(frame_rows, heads_here, HEAD)
    initial = (
        jnp.full((heads_here, frame_rows), -1e30, jnp.float32),
        jnp.zeros((heads_here, frame_rows), jnp.float32),
        jnp.zeros((frame_rows, heads_here, HEAD), jnp.float32),
    )
    pieces = (
        lax.all_gather(projected[1], "ctx", axis=0, tiled=True),
        lax.all_gather(projected[2], "ctx", axis=0, tiled=True),
    )
    key_count = pieces[0].shape[0]
    block_len = 1024 if key_count > 1024 and key_count % 1024 == 0 else key_count
    key_blocks = pieces[0].reshape(key_count // block_len, block_len, heads_here, HEAD)
    value_blocks = pieces[1].reshape(key_count // block_len, block_len, heads_here, HEAD)

    def one_block(running, pieces_now):
        running_max, denominator, weighted = running
        key_block, value_block = pieces_now
        scores = (
            jnp.einsum("qhd,khd->hqk", query_heads, key_block, preferred_element_type=jnp.float32)
            * score_scale
        )
        new_max = jnp.maximum(running_max, jnp.max(scores, axis=-1))
        weights = jnp.exp(scores - new_max[:, :, None])
        rescale = jnp.exp(running_max - new_max)
        denominator = denominator * rescale + jnp.sum(weights, axis=-1)
        added = jnp.einsum(
            "hqk,khd->qhd",
            weights.astype(jnp.bfloat16),
            value_block,
            preferred_element_type=jnp.float32,
        )
        weighted = weighted * jnp.transpose(rescale)[:, :, None] + added
        return ((new_max, denominator, weighted), None)

    result, _ = lax.scan(one_block, initial, (key_blocks, value_blocks))
    running_max, denominator, weighted = result
    context = (
        (weighted / jnp.transpose(denominator)[:, :, None])
        .reshape(frame_rows, local_cols)
        .astype(jnp.bfloat16)
    )
    attn_terms = jnp.dot(context, out_weight, preferred_element_type=jnp.float32)
    summed = lax.psum(attn_terms.astype(jnp.bfloat16), "tp").astype(jnp.float32)
    middle_whole = (whole_rows.astype(jnp.float32) + summed).astype(jnp.bfloat16)
    middle = lax.dynamic_slice_in_dim(
        middle_whole, lax.axis_index("tp") * local_cols, local_cols, 1
    )
    normed_conv = layer_norm(middle_whole, conv_gain)
    halves = jnp.einsum("td,gdc->gtc", normed_conv, glu_weight, preferred_element_type=jnp.float32)
    glu = (halves[0] * jax.nn.sigmoid(halves[1])).astype(jnp.bfloat16)
    reach = depth_kernel.shape[0] // 2
    regrouped = lax.all_to_all(glu, "ctx", split_axis=1, concat_axis=0, tiled=True)
    group_cols = regrouped.shape[1]
    offset_cols = lax.axis_index("ctx") * group_cols
    kernel_part = lax.dynamic_slice_in_dim(depth_kernel, offset_cols, group_cols, 1)
    bias_part = lax.dynamic_slice_in_dim(depth_bias, offset_cols, group_cols, 0)
    padded = jnp.pad(regrouped, ((reach, reach), (0, 0)))
    activated_part = depthwise(padded, kernel_part, bias_part, regrouped.shape[0])
    activated = lax.all_to_all(activated_part, "ctx", split_axis=0, concat_axis=1, tiled=True)
    conv_terms = jnp.dot(activated, proj_weight, preferred_element_type=jnp.float32)
    conv_sum = lax.psum_scatter(
        conv_terms.astype(jnp.bfloat16), "tp", scatter_dimension=1, tiled=True
    ).astype(jnp.float32)
    return (middle.astype(jnp.float32) + conv_sum).astype(jnp.bfloat16)


def pick(table, row, column):
    value = 0
    for index, line in enumerate(table):
        value = value + jnp.where(row == index, line[column], 0)
    return value


def norm_rows(parts, gain, store):
    width = sum(part.shape[-1] for part in parts)
    total = sum(jnp.sum(part, axis=-1, keepdims=True) for part in parts)
    average = total / width
    centered = [part - average for part in parts]
    squares = sum(jnp.sum(part * part, axis=-1, keepdims=True) for part in centered)
    scale = lax.rsqrt(squares / width + 1e-05)
    start = 0
    for index, part in enumerate(centered):
        stop = start + part.shape[-1]
        store(index, (part * scale * gain[:, start:stop]).astype(jnp.bfloat16))
        start = stop


def fused_kernel(
    ctx_size,
    tp_size,
    frames,
    attn_gain,
    qkv,
    out_w,
    conv_gain,
    glu_w,
    depth_k,
    depth_b,
    proj_w,
    out,
    w_qkv,
    w_head,
    w_out,
    w_glu,
    w_proj,
    taps,
    taps32,
    attn_scale,
    conv_scale,
    bias,
    gathered,
    normed,
    q_all,
    k_all,
    k_turned,
    v_all,
    score_rows,
    context_out,
    context_in,
    part32,
    part16,
    pair_in,
    pair_sum,
    peer_in,
    middle,
    glu16,
    halo_low,
    halo_high,
    padded,
    act,
    conv32,
    conv16,
    conv_pair_in,
    conv_keep,
    conv_send,
    conv_peer_in,
    local_sem,
    gather_recv,
    sib_send,
    peer_send,
    up_send,
    down_send,
    side_send,
    ctx_send,
    ctx_recv,
    stage_send,
    stage_recv,
    halo_send,
    halo_recv,
):
    c = lax.axis_index("ctx")
    t = lax.axis_index("tp")
    y = t // 2
    k = t % 2
    sibling = y * 2 + (1 - k)
    peer = (1 - y) * 2 + k
    diagonal = (1 - y) * 2 + (1 - k)
    rows, cols = frames.shape
    step_rows = rows // ROW_CHUNKS

    def remote(source, target, send, receive, **device):
        return pltpu.make_async_remote_copy(
            src_ref=source,
            dst_ref=target,
            send_sem=send,
            recv_sem=receive,
            device_id=device,
            device_id_type=MESH,
        )

    first_col = c * HEAD
    window = jnp.minimum(first_col // 128, (cols - WINDOW) // 128)
    shift = first_col - window * 128
    window_cols = pl.ds(pl.multiple_of(window * 128, 128), WINDOW)

    part_rows = rows // PARTS

    def block(ctx_index, tp_index, part=None):
        if part is None:
            at = pl.ds(pl.multiple_of(ctx_index * rows, 16), rows)
        else:
            at = pl.ds(pl.multiple_of(ctx_index * rows + part * part_rows, 16), part_rows)
        return gathered.at[tp_index, at]

    local = [pltpu.make_async_copy(frames, block(c, t), local_sem.at[0])]
    for i in range(3):
        local.append(
            pltpu.make_async_copy(
                qkv.at[i, :, window_cols],
                w_qkv.at[:, pl.ds(i * WINDOW, WINDOW)],
                local_sem.at[1 + i],
            )
        )
    out_copies = [
        pltpu.make_async_copy(
            out_w.at[pl.ds(head * HEAD, HEAD)],
            w_out.at[pl.ds(head * SLOT, HEAD)],
            local_sem.at[12 + head],
        )
        for head in range(ctx_size)
    ]
    local.append(out_copies[0])
    for i in range(2):
        local.append(
            pltpu.make_async_copy(
                glu_w.at[i], w_glu.at[:, pl.ds(i * cols, cols)], local_sem.at[5 + i]
            )
        )
    local.append(pltpu.make_async_copy(proj_w, w_proj, local_sem.at[7]))
    local.append(pltpu.make_async_copy(depth_k, taps, local_sem.at[8]))
    local.append(pltpu.make_async_copy(conv_gain, conv_scale, local_sem.at[9]))
    local.append(pltpu.make_async_copy(depth_b, bias, local_sem.at[10]))
    local.insert(4, pltpu.make_async_copy(attn_gain, attn_scale, local_sem.at[11]))

    local += out_copies[1:]

    barrier = pltpu.get_barrier_semaphore()
    for other in (sibling, peer):
        pl.semaphore_signal(barrier, inc=1, device_id={"tp": other}, device_id_type=MESH)
    for hop in range(1, ctx_size):
        pl.semaphore_signal(
            barrier, inc=1, device_id={"ctx": (c + hop) % ctx_size}, device_id_type=MESH
        )
    for copy in local:
        copy.start()
    pl.semaphore_wait(barrier, 2 + ctx_size - 1)

    def own_part(part):
        return frames.at[pl.ds(part * part_rows, part_rows)]

    def to_peer(index, part, source):
        return remote(
            source,
            block(index, t, part),
            peer_send.at[index, part],
            gather_recv.at[index, t, part],
            tp=peer,
        )

    def to_sibling(index, half, part, source):
        owner = half * 2 + k
        return remote(
            source,
            block(index, owner, part),
            sib_send.at[index, half, part],
            gather_recv.at[index, owner, part],
            tp=sibling,
        )

    def up(index, part, source):
        return remote(
            source,
            block(index, t, part),
            up_send.at[index, part],
            gather_recv.at[index, t, part],
            ctx=c + 1,
        )

    def down(index, part, source):
        return remote(
            source,
            block(index, t, part),
            down_send.at[index, part],
            gather_recv.at[index, t, part],
            ctx=c - 1,
        )

    end = ctx_size - 1
    late = PARTS - 1

    def side_up():
        here = block(0, peer, late)
        return remote(here, here, side_send.at[0], gather_recv.at[0, peer, late], ctx=c + 1)

    def side_down():
        here = block(end, peer, late)
        return remote(here, here, side_send.at[1], gather_recv.at[end, peer, late], ctx=c - 1)

    def arrived(index, owner, part):
        here = block(index, owner, part)
        remote(
            here, here, peer_send.at[index, part], gather_recv.at[index, owner, part], tp=peer
        ).wait_recv()

    has_up = c + 1 < ctx_size
    has_down = c > 0

    for part in range(PARTS):
        source = own_part(part)
        pl.when(has_up)(lambda: up(c, part, source).start())
        pl.when(has_down)(lambda: down(c, part, source).start())
        to_peer(c, part, source).start()
        to_sibling(c, y, part, source).start()

    order = []
    for place in range(ctx_size):
        line = [place]
        for hop in range(1, ctx_size):
            line += [i for i in (place - hop, place + hop) if 0 <= i < ctx_size]
        order.append(line)

    select_row = lax.broadcasted_iota(jnp.int32, (WINDOW, SLOT), 0)
    select_col = lax.broadcasted_iota(jnp.int32, (WINDOW, SLOT), 1)
    select = ((select_row == select_col + shift) & (select_col < HEAD)).astype(jnp.bfloat16)

    for i in range(3):
        local[1 + i].wait()
        w_head[:, i * SLOT : (i + 1) * SLOT] = jnp.dot(
            w_qkv[:, i * WINDOW : (i + 1) * WINDOW], select, preferred_element_type=jnp.float32
        ).astype(jnp.bfloat16)

    def project(place):
        index = pick(order, c, place)
        start = pl.multiple_of(index * rows, 16)
        sub = part_rows // 2
        for part in range(PARTS):
            arrived(index, sibling, part)
            arrived(index, diagonal, part)
            for step in range(2 * part, 2 * part + 2):
                at = pl.ds(pl.multiple_of(start + step * sub, 16), sub)

                def store(piece, value):
                    normed[pl.ds(step * sub, sub), piece * cols : (piece + 1) * cols] = value

                norm_rows(
                    [gathered[i, at, :].astype(jnp.float32) for i in range(tp_size)],
                    attn_scale[...].reshape(1, -1),
                    store,
                )
        here = pl.ds(start, rows)
        projected = jnp.dot(
            normed[...], w_head[...], preferred_element_type=jnp.float32
        ).astype(jnp.bfloat16)
        for step in range(ROW_CHUNKS):
            at = pl.ds(pl.multiple_of(index * step_rows, 16), step_rows)
            q_all[step, at, :] = projected[step * step_rows : (step + 1) * step_rows, :SLOT]
        k_all[here, :] = projected[:, SLOT : 2 * SLOT]
        v_all[here, :] = projected[:, 2 * SLOT :]

    def pass_on(hop):
        for part in range(PARTS):

            @pl.when(c >= hop)
            def _():
                index = c - hop
                arrived(index, t, part)
                source = block(index, t, part)
                pl.when(has_up)(lambda: up(index, part, source).start())
                if part == late:
                    pl.when(index > 0)(lambda: to_peer(index, part, source).start())
                else:
                    to_peer(index, part, source).start()
                to_sibling(index, y, part, source).start()

            @pl.when(c + hop < ctx_size)
            def _():
                index = c + hop
                arrived(index, t, part)
                source = block(index, t, part)
                pl.when(has_down)(lambda: down(index, part, source).start())
                if part == late:
                    pl.when(index < end)(lambda: to_peer(index, part, source).start())
                else:
                    to_peer(index, part, source).start()
                to_sibling(index, y, part, source).start()

    def pass_side(hop):
        @pl.when(c == hop)
        def _():
            arrived(0, peer, late)
            pl.when(has_up)(lambda: side_up().start())
            to_sibling(0, 1 - y, late, block(0, peer, late)).start()

        @pl.when(c + hop == end)
        def _():
            arrived(end, peer, late)
            pl.when(has_down)(lambda: side_down().start())
            to_sibling(end, 1 - y, late, block(end, peer, late)).start()

    def from_peer(place):
        index = pick(order, c, place)

        def take(part):
            arrived(index, peer, part)
            to_sibling(index, 1 - y, part, block(index, peer, part)).start()

        for part in range(PARTS):
            if part == late and place:
                pl.when((index > 0) & (index < end))(lambda: take(part))
            else:
                take(part)
        if not place:
            pl.when(c == 0)(lambda: side_up().start())
            pl.when(c == end)(lambda: side_down().start())

    pass_on(1)
    from_peer(0)
    pass_on(2)
    pass_side(1)
    from_peer(1)
    local[0].wait()
    local[4].wait()
    project(0)
    for place in range(2, ctx_size):
        last = place == ctx_size - 1
        if not last:
            pass_on(place + 1)
        else:
            project(place - 1)
        pass_side(place)
        from_peer(place)
        if not last:
            project(place - 1)
    project(ctx_size - 1)

    score_scale = 1.0 / math.sqrt(HEAD)

    def chunk(step):
        return pl.ds(step * step_rows, step_rows)

    def head_slot(head):
        return pl.ds(pl.multiple_of(head * SLOT, SLOT), SLOT)

    def context_copy(index, step):
        return remote(
            context_out.at[index, chunk(step)],
            context_in.at[chunk(step), head_slot(c)],
            ctx_send.at[index, step],
            ctx_recv.at[c, step],
            ctx=index,
        )

    k_turned[...] = k_all[...].T

    def attend(step, places):
        indices = [pick(order, c, place) for place in places]
        rounded, denominators = [], []
        for index in indices:
            at = pl.ds(pl.multiple_of(index * step_rows, 16), step_rows)
            scores = score_rows[at, :] * score_scale
            weights = jnp.exp(scores - jnp.max(scores, axis=-1, keepdims=True))
            denominators.append(jnp.sum(weights, axis=-1, keepdims=True))
            rounded.append(weights.astype(jnp.bfloat16))
        weighted = jnp.dot(
            jnp.concatenate(rounded, axis=0), v_all[...], preferred_element_type=jnp.float32
        )
        for i, (place, index) in enumerate(zip(places, indices)):
            piece = weighted[i * step_rows : (i + 1) * step_rows] / denominators[i]
            if place:
                context_out[index, chunk(step), :] = piece.astype(jnp.bfloat16)
                context_copy(index, step).start()
            else:
                context_in[chunk(step), head_slot(c)] = piece.astype(jnp.bfloat16)

    farthest = list(reversed(range(ctx_size)))
    for step in range(ROW_CHUNKS):
        score_rows[...] = jnp.dot(
            q_all[step], k_turned[...], preferred_element_type=jnp.float32
        )
        for first in range(0, ctx_size, 2):
            attend(step, farthest[first : first + 2])
    for copy in out_copies:
        copy.wait()
    for head in range(ctx_size):
        w_out[head * SLOT + HEAD : (head + 1) * SLOT, :] = jnp.zeros(
            (SLOT - HEAD, w_out.shape[1]), jnp.bfloat16
        )

    mine = pl.ds(2 * k, 2)
    others = pl.ds(2 * (1 - k), 2)

    def stage(kind, step, source, target, device):
        return remote(
            source, target, stage_send.at[kind, step], stage_recv.at[kind, step], tp=device
        )

    def pair_copy(step):
        return stage(0, step, part16.at[others, chunk(step)], pair_in.at[:, chunk(step)], sibling)

    def peer_copy(step):
        return stage(1, step, pair_sum.at[:, chunk(step)], peer_in.at[:, chunk(step)], peer)

    def middle_copy(step, half):
        ref = middle.at[half, chunk(step)]
        return stage(2, step, ref, ref, sibling)

    for step in range(ROW_CHUNKS):
        for hop in range(1, ctx_size):
            index = (c + hop) % ctx_size
            here = context_in.at[chunk(step), head_slot(index)]
            remote(here, here, ctx_send.at[index, step], ctx_recv.at[index, step], ctx=index).wait_recv()
        terms = jnp.dot(
            context_in[chunk(step), :], w_out[...], preferred_element_type=jnp.float32
        )
        for i in range(tp_size):
            piece = terms[:, i * cols : (i + 1) * cols]
            part32[i, chunk(step), :] = piece
            part16[i, chunk(step), :] = piece.astype(jnp.bfloat16)
        pair_copy(step).start()
    for step in range(ROW_CHUNKS):
        pair_copy(step).wait_recv()
        pair_sum[:, chunk(step), :] = (
            part32[mine, chunk(step), :] + pair_in[:, chunk(step), :].astype(jnp.float32)
        ).astype(jnp.bfloat16)
        peer_copy(step).start()

    for i in range(6, 12):
        local[i].wait()
    taps32[...] = taps[...].astype(jnp.float32)

    def halo_up():
        return remote(
            glu16.at[pl.ds(rows - HALO, HALO)], halo_low, halo_send.at[0], halo_recv.at[0], ctx=c + 1
        )

    def halo_down():
        return remote(glu16.at[pl.ds(0, HALO)], halo_high, halo_send.at[1], halo_recv.at[1], ctx=c - 1)

    for step in range(ROW_CHUNKS):
        peer_copy(step).wait_recv()
        own = pl.ds(pl.multiple_of(c * rows + step * step_rows, 16), step_rows)
        summed = pair_sum[:, chunk(step), :].astype(jnp.float32) + peer_in[
            :, chunk(step), :
        ].astype(jnp.float32)
        middle[mine, chunk(step), :] = (
            gathered[mine, own, :].astype(jnp.float32) + summed
        ).astype(jnp.bfloat16)
        middle_copy(step, mine).start()
        middle_copy(step, others).wait_recv()

        def store(part, value):
            normed[chunk(step), part * cols : (part + 1) * cols] = value

        norm_rows(
            [middle[i, chunk(step), :].astype(jnp.float32) for i in range(tp_size)],
            conv_scale[...].reshape(1, -1),
            store,
        )
        halves = jnp.dot(normed[chunk(step), :], w_glu[...], preferred_element_type=jnp.float32)
        glu = (halves[:, :cols] * jax.nn.sigmoid(halves[:, cols:])).astype(jnp.bfloat16)
        glu16[chunk(step), :] = glu
        padded[HALO + step * step_rows : HALO + (step + 1) * step_rows, :] = glu.astype(jnp.float32)
        if step == 0:
            pl.when(has_down)(lambda: halo_down().start())
        if step == ROW_CHUNKS - 1:
            pl.when(has_up)(lambda: halo_up().start())

    def edge_low():
        padded[0:HALO, :] = jnp.zeros((HALO, cols), jnp.float32)

        @pl.when(has_down)
        def _():
            halo_up().wait_recv()
            padded[0:HALO, :] = halo_low[...].astype(jnp.float32)

    def edge_high():
        padded[HALO + rows :, :] = jnp.zeros((HALO, cols), jnp.float32)

        @pl.when(has_up)
        def _():
            halo_down().wait_recv()
            padded[HALO + rows :, :] = halo_high[...].astype(jnp.float32)

    def conv_pair(step):
        return stage(
            3, step, conv16.at[others, chunk(step)], conv_pair_in.at[:, chunk(step)], sibling
        )

    def conv_peer(step):
        return stage(4, step, conv_send.at[chunk(step)], conv_peer_in.at[chunk(step)], peer)

    tap_count = taps32.shape[0]
    first = HALO - tap_count // 2
    last_first = list(reversed(range(ROW_CHUNKS)))
    for step in last_first:
        if step == ROW_CHUNKS - 1:
            edge_high()
        if step == 0:
            edge_low()
        for lane in range(0, cols, 128):
            lanes = slice(lane, lane + 128)
            total = jnp.zeros((step_rows, 128), jnp.float32)
            for tap in range(tap_count):
                at = step * step_rows + first + tap
                total = total + padded[at : at + step_rows, lanes] * taps32[tap : tap + 1, lanes]
            total = total + bias[lanes].reshape(1, -1)
            act[chunk(step), lanes] = (total / (1.0 + jnp.exp(-total))).astype(jnp.bfloat16)
        terms = jnp.dot(act[chunk(step), :], w_proj[...], preferred_element_type=jnp.float32)
        for i in range(tp_size):
            piece = terms[:, i * cols : (i + 1) * cols]
            slot = (i % 2) * 2 + i // 2
            conv32[slot, chunk(step), :] = piece
            conv16[slot, chunk(step), :] = piece.astype(jnp.bfloat16)
        conv_pair(step).start()
    for step in last_first:
        conv_pair(step).wait_recv()
        conv_send[chunk(step), :] = (
            conv32[2 * k + 1 - y, chunk(step), :]
            + conv_pair_in[1 - y, chunk(step), :].astype(jnp.float32)
        ).astype(jnp.bfloat16)
        conv_peer(step).start()
        conv_keep[chunk(step), :] = (
            conv32[2 * k + y, chunk(step), :]
            + conv_pair_in[y, chunk(step), :].astype(jnp.float32)
            + middle[t, chunk(step), :].astype(jnp.float32)
        )
    for step in last_first:
        conv_peer(step).wait_recv()
        out[chunk(step), :] = (
            conv_keep[chunk(step), :] + conv_peer_in[chunk(step), :].astype(jnp.float32)
        ).astype(jnp.bfloat16)

    for place in range(ctx_size):
        for part in range(PARTS):
            index = pick(order, c, place)
            source = block(index, t, part)
            pl.when(has_up & (index <= c))(lambda: up(index, part, source).wait_send())
            pl.when(has_down & (index >= c))(lambda: down(index, part, source).wait_send())
            if part == late:
                crossed = (index == c) | ((index > 0) & (index < end))
                pl.when(crossed)(lambda: to_peer(index, part, source).wait_send())
            else:
                to_peer(index, part, source).wait_send()
            to_sibling(index, y, part, source).wait_send()
            to_sibling(index, 1 - y, part, source).wait_send()
    pl.when(has_up)(lambda: side_up().wait_send())
    pl.when(has_down)(lambda: side_down().wait_send())
    for hop in range(1, ctx_size):
        for step in range(ROW_CHUNKS):
            context_copy((c + hop) % ctx_size, step).wait_send()
    for step in range(ROW_CHUNKS):
        pair_copy(step).wait_send()
        peer_copy(step).wait_send()
        middle_copy(step, mine).wait_send()
        conv_pair(step).wait_send()
        conv_peer(step).wait_send()
    pl.when(has_up)(lambda: halo_up().wait_send())
    pl.when(has_down)(lambda: halo_down().wait_send())


def fused(
    ctx_size,
    tp_size,
    frames,
    attn_gain,
    query_key_value,
    out_weight,
    conv_gain,
    glu_weight,
    depth_kernel,
    depth_bias,
    proj_weight,
):
    rows, cols = frames.shape
    width = cols * tp_size
    all_rows = rows * ctx_size
    taps = depth_kernel.shape[0]
    wide, narrow = jnp.float32, jnp.bfloat16
    vmem = pl.BlockSpec(memory_space=pltpu.VMEM)
    away = pl.BlockSpec(memory_space=pltpu.HBM)
    dma = pltpu.SemaphoreType.DMA
    return pl.pallas_call(
        functools.partial(fused_kernel, ctx_size, tp_size),
        out_shape=jax.ShapeDtypeStruct((rows, cols), narrow),
        in_specs=[away] * 9,
        out_specs=vmem,
        scratch_shapes=[
            pltpu.VMEM((width, 3 * WINDOW), narrow),
            pltpu.VMEM((width, 3 * SLOT), narrow),
            pltpu.VMEM((ctx_size * SLOT, width), narrow),
            pltpu.VMEM((width, 2 * cols), narrow),
            pltpu.VMEM((cols, width), narrow),
            pltpu.VMEM((taps, cols), narrow),
            pltpu.VMEM((taps, cols), wide),
            pltpu.VMEM((width,), wide),
            pltpu.VMEM((width,), wide),
            pltpu.VMEM((cols,), wide),
            pltpu.VMEM((tp_size, all_rows, cols), narrow),
            pltpu.VMEM((rows, width), narrow),
            pltpu.VMEM((ROW_CHUNKS, all_rows // ROW_CHUNKS, SLOT), narrow),
            pltpu.VMEM((all_rows, SLOT), narrow),
            pltpu.VMEM((SLOT, all_rows), narrow),
            pltpu.VMEM((all_rows, SLOT), narrow),
            pltpu.VMEM((all_rows // ROW_CHUNKS, all_rows), wide),
            pltpu.VMEM((ctx_size, rows, SLOT), narrow),
            pltpu.VMEM((rows, ctx_size * SLOT), narrow),
            pltpu.VMEM((tp_size, rows, cols), wide),
            pltpu.VMEM((tp_size, rows, cols), narrow),
            pltpu.VMEM((2, rows, cols), narrow),
            pltpu.VMEM((2, rows, cols), narrow),
            pltpu.VMEM((2, rows, cols), narrow),
            pltpu.VMEM((tp_size, rows, cols), narrow),
            pltpu.VMEM((rows, cols), narrow),
            pltpu.VMEM((HALO, cols), narrow),
            pltpu.VMEM((HALO, cols), narrow),
            pltpu.VMEM((rows + 2 * HALO, cols), wide),
            pltpu.VMEM((rows, cols), narrow),
            pltpu.VMEM((tp_size, rows, cols), wide),
            pltpu.VMEM((tp_size, rows, cols), narrow),
            pltpu.VMEM((2, rows, cols), narrow),
            pltpu.VMEM((rows, cols), wide),
            pltpu.VMEM((rows, cols), narrow),
            pltpu.VMEM((rows, cols), narrow),
            dma((12 + ctx_size,)),
            dma((ctx_size, tp_size, PARTS)),
            dma((ctx_size, 2, PARTS)),
            dma((ctx_size, PARTS)),
            dma((ctx_size, PARTS)),
            dma((ctx_size, PARTS)),
            dma((2,)),
            dma((ctx_size, ROW_CHUNKS)),
            dma((ctx_size, ROW_CHUNKS)),
            dma((5, ROW_CHUNKS)),
            dma((5, ROW_CHUNKS)),
            dma((2,)),
            dma((2,)),
        ],
        compiler_params=pltpu.CompilerParams(
            collective_id=0, has_side_effects=True, vmem_limit_bytes=62 * 1024 * 1024
        ),
    )(
        frames,
        attn_gain,
        query_key_value,
        out_weight,
        conv_gain,
        glu_weight,
        depth_kernel,
        depth_bias,
        proj_weight,
    )


def solution(mesh):
    in_specs = (
        P(("batch", "ctx"), "tp"),
        P(),
        P(None, None, "tp"),
        P("tp", None),
        P(),
        P(None, None, "tp"),
        P(None, "tp"),
        P("tp"),
        P("tp", None),
    )
    out_specs = P(("batch", "ctx"), "tp")
    ctx_size, tp_size = mesh.shape["ctx"], mesh.shape["tp"]

    def body(frames, attn_gain, query_key_value, *rest):
        one_head_each = ctx_size * HEAD == query_key_value.shape[2]
        even = frames.shape[0] % (16 * ROW_CHUNKS * PARTS) == 0
        if tp_size == 4 and one_head_each and ctx_size > 2 and even:
            return fused(ctx_size, tp_size, frames, attn_gain, query_key_value, *rest)
        return per_device(frames, attn_gain, query_key_value, *rest)

    return jax.shard_map(
        body, mesh=mesh, in_specs=in_specs, out_specs=out_specs, check_vma=False
    )
```

```python
import functools
import math

import jax
import jax.numpy as jnp
from jax import lax
from jax.experimental import pallas as pl
from jax.experimental.pallas import tpu as pltpu
from jax.sharding import PartitionSpec as P

HEAD = 96
HALO = 16
ROW_CHUNKS = 2
PARTS = 2
WINDOW = 256
SLOT = 128
MESH = pl.DeviceIdType.MESH


def layer_norm(inputs, gain):
    inputs = inputs.astype(jnp.float32)
    average = jnp.mean(inputs, axis=-1, keepdims=True)
    centered = inputs - average
    variance = jnp.mean(centered * centered, axis=-1, keepdims=True)
    return (centered * lax.rsqrt(variance + 1e-05) * gain).astype(jnp.bfloat16)


def depthwise(padded, kernel, bias, count):
    convolved = jnp.zeros((count, padded.shape[1]), jnp.float32)
    for kernel_tap in range(kernel.shape[0]):
        convolved = convolved + padded[kernel_tap : kernel_tap + count].astype(
            jnp.float32
        ) * kernel[kernel_tap].astype(jnp.float32)
    return jax.nn.silu(convolved + bias).astype(jnp.bfloat16)


def per_device(
    frames,
    attn_gain,
    query_key_value,
    out_weight,
    conv_gain,
    glu_weight,
    depth_kernel,
    depth_bias,
    proj_weight,
):
    frame_rows = frames.shape[0]
    local_cols = frames.shape[1]
    heads_here = query_key_value.shape[2] // HEAD
    whole_rows = lax.all_gather(frames, "tp", axis=1, tiled=True)
    normed = layer_norm(whole_rows, attn_gain)
    projected = jnp.einsum(
        "td,gdc->gtc", normed, query_key_value, preferred_element_type=jnp.float32
    ).astype(jnp.bfloat16)
    score_scale = 1.0 / math.sqrt(HEAD)
    query_heads = projected[0].reshape(frame_rows, heads_here, HEAD)
    initial = (
        jnp.full((heads_here, frame_rows), -1e30, jnp.float32),
        jnp.zeros((heads_here, frame_rows), jnp.float32),
        jnp.zeros((frame_rows, heads_here, HEAD), jnp.float32),
    )
    pieces = (
        lax.all_gather(projected[1], "ctx", axis=0, tiled=True),
        lax.all_gather(projected[2], "ctx", axis=0, tiled=True),
    )
    key_count = pieces[0].shape[0]
    block_len = 1024 if key_count > 1024 and key_count % 1024 == 0 else key_count
    key_blocks = pieces[0].reshape(key_count // block_len, block_len, heads_here, HEAD)
    value_blocks = pieces[1].reshape(key_count // block_len, block_len, heads_here, HEAD)

    def one_block(running, pieces_now):
        running_max, denominator, weighted = running
        key_block, value_block = pieces_now
        scores = (
            jnp.einsum("qhd,khd->hqk", query_heads, key_block, preferred_element_type=jnp.float32)
            * score_scale
        )
        new_max = jnp.maximum(running_max, jnp.max(scores, axis=-1))
        weights = jnp.exp(scores - new_max[:, :, None])
        rescale = jnp.exp(running_max - new_max)
        denominator = denominator * rescale + jnp.sum(weights, axis=-1)
        added = jnp.einsum(
            "hqk,khd->qhd",
            weights.astype(jnp.bfloat16),
            value_block,
            preferred_element_type=jnp.float32,
        )
        weighted = weighted * jnp.transpose(rescale)[:, :, None] + added
        return ((new_max, denominator, weighted), None)

    result, _ = lax.scan(one_block, initial, (key_blocks, value_blocks))
    running_max, denominator, weighted = result
    context = (
        (weighted / jnp.transpose(denominator)[:, :, None])
        .reshape(frame_rows, local_cols)
        .astype(jnp.bfloat16)
    )
    attn_terms = jnp.dot(context, out_weight, preferred_element_type=jnp.float32)
    summed = lax.psum(attn_terms.astype(jnp.bfloat16), "tp").astype(jnp.float32)
    middle_whole = (whole_rows.astype(jnp.float32) + summed).astype(jnp.bfloat16)
    middle = lax.dynamic_slice_in_dim(
        middle_whole, lax.axis_index("tp") * local_cols, local_cols, 1
    )
    normed_conv = layer_norm(middle_whole, conv_gain)
    halves = jnp.einsum("td,gdc->gtc", normed_conv, glu_weight, preferred_element_type=jnp.float32)
    glu = (halves[0] * jax.nn.sigmoid(halves[1])).astype(jnp.bfloat16)
    reach = depth_kernel.shape[0] // 2
    regrouped = lax.all_to_all(glu, "ctx", split_axis=1, concat_axis=0, tiled=True)
    group_cols = regrouped.shape[1]
    offset_cols = lax.axis_index("ctx") * group_cols
    kernel_part = lax.dynamic_slice_in_dim(depth_kernel, offset_cols, group_cols, 1)
    bias_part = lax.dynamic_slice_in_dim(depth_bias, offset_cols, group_cols, 0)
    padded = jnp.pad(regrouped, ((reach, reach), (0, 0)))
    activated_part = depthwise(padded, kernel_part, bias_part, regrouped.shape[0])
    activated = lax.all_to_all(activated_part, "ctx", split_axis=0, concat_axis=1, tiled=True)
    conv_terms = jnp.dot(activated, proj_weight, preferred_element_type=jnp.float32)
    conv_sum = lax.psum_scatter(
        conv_terms.astype(jnp.bfloat16), "tp", scatter_dimension=1, tiled=True
    ).astype(jnp.float32)
    return (middle.astype(jnp.float32) + conv_sum).astype(jnp.bfloat16)


def pick(table, row, column):
    value = 0
    for index, line in enumerate(table):
        value = value + jnp.where(row == index, line[column], 0)
    return value


def norm_rows(parts, gain, store):
    width = sum(part.shape[-1] for part in parts)
    total = sum(jnp.sum(part, axis=-1, keepdims=True) for part in parts)
    average = total / width
    centered = [part - average for part in parts]
    squares = sum(jnp.sum(part * part, axis=-1, keepdims=True) for part in centered)
    scale = lax.rsqrt(squares / width + 1e-05)
    start = 0
    for index, part in enumerate(centered):
        stop = start + part.shape[-1]
        store(index, (part * scale * gain[:, start:stop]).astype(jnp.bfloat16))
        start = stop


def fused_kernel(
    ctx_size,
    tp_size,
    frames,
    attn_gain,
    qkv,
    out_w,
    conv_gain,
    glu_w,
    depth_k,
    depth_b,
    proj_w,
    out,
    w_qkv,
    w_head,
    w_out,
    w_glu,
    w_proj,
    taps,
    taps32,
    attn_scale,
    conv_scale,
    bias,
    gathered,
    normed,
    q_all,
    k_all,
    k_turned,
    v_all,
    score_rows,
    context_out,
    context_in,
    part32,
    part16,
    pair_in,
    pair_sum,
    peer_in,
    middle,
    glu16,
    halo_low,
    halo_high,
    padded,
    act,
    conv32,
    conv16,
    conv_pair_in,
    conv_keep,
    conv_send,
    conv_peer_in,
    local_sem,
    gather_recv,
    sib_send,
    peer_send,
    along_send,
    ctx_send,
    ctx_recv,
    stage_send,
    stage_recv,
    halo_send,
    halo_recv,
):
    c = lax.axis_index("ctx")
    t = lax.axis_index("tp")
    y = t // 2
    k = t % 2
    sibling = y * 2 + (1 - k)
    peer = (1 - y) * 2 + k
    diagonal = (1 - y) * 2 + (1 - k)
    rows, cols = frames.shape
    step_rows = rows // ROW_CHUNKS

    def remote(source, target, send, receive, **device):
        return pltpu.make_async_remote_copy(
            src_ref=source,
            dst_ref=target,
            send_sem=send,
            recv_sem=receive,
            device_id=device,
            device_id_type=MESH,
        )

    first_col = c * HEAD
    window = jnp.minimum(first_col // 128, (cols - WINDOW) // 128)
    shift = first_col - window * 128
    window_cols = pl.ds(pl.multiple_of(window * 128, 128), WINDOW)

    part_rows = rows // PARTS

    def block(ctx_index, tp_index, part=None):
        if part is None:
            at = pl.ds(pl.multiple_of(ctx_index * rows, 16), rows)
        else:
            at = pl.ds(pl.multiple_of(ctx_index * rows + part * part_rows, 16), part_rows)
        return gathered.at[tp_index, at]

    local = [pltpu.make_async_copy(frames, block(c, t), local_sem.at[0])]
    for i in range(3):
        local.append(
            pltpu.make_async_copy(
                qkv.at[i, :, window_cols],
                w_qkv.at[:, pl.ds(i * WINDOW, WINDOW)],
                local_sem.at[1 + i],
            )
        )
    out_copies = [
        pltpu.make_async_copy(
            out_w.at[pl.ds(head * HEAD, HEAD)],
            w_out.at[pl.ds(head * SLOT, HEAD)],
            local_sem.at[12 + head],
        )
        for head in range(ctx_size)
    ]
    local.append(out_copies[0])
    for i in range(2):
        local.append(
            pltpu.make_async_copy(
                glu_w.at[i], w_glu.at[:, pl.ds(i * cols, cols)], local_sem.at[5 + i]
            )
        )
    local.append(pltpu.make_async_copy(proj_w, w_proj, local_sem.at[7]))
    local.append(pltpu.make_async_copy(depth_k, taps, local_sem.at[8]))
    local.append(pltpu.make_async_copy(conv_gain, conv_scale, local_sem.at[9]))
    local.append(pltpu.make_async_copy(depth_b, bias, local_sem.at[10]))
    local.insert(4, pltpu.make_async_copy(attn_gain, attn_scale, local_sem.at[11]))

    local += out_copies[1:]

    barrier = pltpu.get_barrier_semaphore()
    for other in (sibling, peer):
        pl.semaphore_signal(barrier, inc=1, device_id={"tp": other}, device_id_type=MESH)
    for hop in range(1, ctx_size):
        pl.semaphore_signal(
            barrier, inc=1, device_id={"ctx": (c + hop) % ctx_size}, device_id_type=MESH
        )
    for copy in local:
        copy.start()
    pl.semaphore_wait(barrier, 2 + ctx_size - 1)

    def own_part(part):
        return frames.at[pl.ds(part * part_rows, part_rows)]

    def to_peer(index, part, source):
        return remote(
            source,
            block(index, t, part),
            peer_send.at[index, part],
            gather_recv.at[index, t, part],
            tp=peer,
        )

    def to_sibling(index, half, part, source):
        owner = half * 2 + k
        return remote(
            source,
            block(index, owner, part),
            sib_send.at[index, half, part],
            gather_recv.at[index, owner, part],
            tp=sibling,
        )

    def along(index, part):
        return remote(
            own_part(part),
            block(c, t, part),
            along_send.at[index, part],
            gather_recv.at[c, t, part],
            ctx=index,
        )

    def arrived(index, owner, part):
        here = block(index, owner, part)
        remote(
            here, here, peer_send.at[index, part], gather_recv.at[index, owner, part], tp=peer
        ).wait_recv()

    has_up = c + 1 < ctx_size
    has_down = c > 0

    for part in range(PARTS):
        to_peer(c, part, own_part(part)).start()
        to_sibling(c, y, part, own_part(part)).start()
    for hop in range(1, ctx_size):
        for part in range(PARTS):
            pl.when(c >= hop)(lambda: along(c - hop, part).start())
            pl.when(c + hop < ctx_size)(lambda: along(c + hop, part).start())

    order = []
    for place in range(ctx_size):
        line = [place]
        for hop in range(1, ctx_size):
            line += [i for i in (place - hop, place + hop) if 0 <= i < ctx_size]
        order.append(line)

    select_row = lax.broadcasted_iota(jnp.int32, (WINDOW, SLOT), 0)
    select_col = lax.broadcasted_iota(jnp.int32, (WINDOW, SLOT), 1)
    select = ((select_row == select_col + shift) & (select_col < HEAD)).astype(jnp.bfloat16)

    for i in range(3):
        local[1 + i].wait()
        w_head[:, i * SLOT : (i + 1) * SLOT] = jnp.dot(
            w_qkv[:, i * WINDOW : (i + 1) * WINDOW], select, preferred_element_type=jnp.float32
        ).astype(jnp.bfloat16)

    def project(place):
        index = pick(order, c, place)
        start = pl.multiple_of(index * rows, 16)
        sub = part_rows // 2
        for part in range(PARTS):
            arrived(index, sibling, part)
            arrived(index, diagonal, part)
            for step in range(2 * part, 2 * part + 2):
                at = pl.ds(pl.multiple_of(start + step * sub, 16), sub)

                def store(piece, value):
                    normed[pl.ds(step * sub, sub), piece * cols : (piece + 1) * cols] = value

                norm_rows(
                    [gathered[i, at, :].astype(jnp.float32) for i in range(tp_size)],
                    attn_scale[...].reshape(1, -1),
                    store,
                )
        here = pl.ds(start, rows)
        projected = jnp.dot(
            normed[...], w_head[...], preferred_element_type=jnp.float32
        ).astype(jnp.bfloat16)
        for step in range(ROW_CHUNKS):
            at = pl.ds(pl.multiple_of(index * step_rows, 16), step_rows)
            q_all[step, at, :] = projected[step * step_rows : (step + 1) * step_rows, :SLOT]
        k_all[here, :] = projected[:, SLOT : 2 * SLOT]
        v_all[here, :] = projected[:, 2 * SLOT :]

    def pass_on(place):
        index = pick(order, c, place)
        for part in range(PARTS):
            arrived(index, t, part)
            source = block(index, t, part)
            to_peer(index, part, source).start()
            to_sibling(index, y, part, source).start()

    def from_peer(place):
        index = pick(order, c, place)
        for part in range(PARTS):
            arrived(index, peer, part)
            to_sibling(index, 1 - y, part, block(index, peer, part)).start()

    from_peer(0)
    pass_on(1)
    pass_on(2)
    from_peer(1)
    local[0].wait()
    local[4].wait()
    project(0)
    for place in range(2, ctx_size):
        last = place == ctx_size - 1
        if not last:
            pass_on(place + 1)
        else:
            project(place - 1)
        from_peer(place)
        if not last:
            project(place - 1)
    project(ctx_size - 1)

    score_scale = 1.0 / math.sqrt(HEAD)

    def chunk(step):
        return pl.ds(step * step_rows, step_rows)

    def head_slot(head):
        return pl.ds(pl.multiple_of(head * SLOT, SLOT), SLOT)

    def context_copy(index, step):
        return remote(
            context_out.at[index, chunk(step)],
            context_in.at[chunk(step), head_slot(c)],
            ctx_send.at[index, step],
            ctx_recv.at[c, step],
            ctx=index,
        )

    k_turned[...] = k_all[...].T

    def attend(step, places):
        indices = [pick(order, c, place) for place in places]
        rounded, denominators = [], []
        for index in indices:
            at = pl.ds(pl.multiple_of(index * step_rows, 16), step_rows)
            scores = score_rows[at, :] * score_scale
            weights = jnp.exp(scores - jnp.max(scores, axis=-1, keepdims=True))
            denominators.append(jnp.sum(weights, axis=-1, keepdims=True))
            rounded.append(weights.astype(jnp.bfloat16))
        weighted = jnp.dot(
            jnp.concatenate(rounded, axis=0), v_all[...], preferred_element_type=jnp.float32
        )
        for i, (place, index) in enumerate(zip(places, indices)):
            piece = weighted[i * step_rows : (i + 1) * step_rows] / denominators[i]
            if place:
                context_out[index, chunk(step), :] = piece.astype(jnp.bfloat16)
                context_copy(index, step).start()
            else:
                context_in[chunk(step), head_slot(c)] = piece.astype(jnp.bfloat16)

    farthest = list(reversed(range(ctx_size)))
    for step in range(ROW_CHUNKS):
        score_rows[...] = jnp.dot(
            q_all[step], k_turned[...], preferred_element_type=jnp.float32
        )
        for first in range(0, ctx_size, 2):
            attend(step, farthest[first : first + 2])
    for copy in out_copies:
        copy.wait()
    for head in range(ctx_size):
        w_out[head * SLOT + HEAD : (head + 1) * SLOT, :] = jnp.zeros(
            (SLOT - HEAD, w_out.shape[1]), jnp.bfloat16
        )

    mine = pl.ds(2 * k, 2)
    others = pl.ds(2 * (1 - k), 2)

    def stage(kind, step, source, target, device):
        return remote(
            source, target, stage_send.at[kind, step], stage_recv.at[kind, step], tp=device
        )

    def pair_copy(step):
        return stage(0, step, part16.at[others, chunk(step)], pair_in.at[:, chunk(step)], sibling)

    def peer_copy(step):
        return stage(1, step, pair_sum.at[:, chunk(step)], peer_in.at[:, chunk(step)], peer)

    def middle_copy(step, half):
        ref = middle.at[half, chunk(step)]
        return stage(2, step, ref, ref, sibling)

    for step in range(ROW_CHUNKS):
        for hop in range(1, ctx_size):
            index = (c + hop) % ctx_size
            here = context_in.at[chunk(step), head_slot(index)]
            remote(here, here, ctx_send.at[index, step], ctx_recv.at[index, step], ctx=index).wait_recv()
        terms = jnp.dot(
            context_in[chunk(step), :], w_out[...], preferred_element_type=jnp.float32
        )
        for i in range(tp_size):
            piece = terms[:, i * cols : (i + 1) * cols]
            part32[i, chunk(step), :] = piece
            part16[i, chunk(step), :] = piece.astype(jnp.bfloat16)
        pair_copy(step).start()
    for step in range(ROW_CHUNKS):
        pair_copy(step).wait_recv()
        pair_sum[:, chunk(step), :] = (
            part32[mine, chunk(step), :] + pair_in[:, chunk(step), :].astype(jnp.float32)
        ).astype(jnp.bfloat16)
        peer_copy(step).start()

    for i in range(6, 12):
        local[i].wait()
    taps32[...] = taps[...].astype(jnp.float32)

    def halo_up():
        return remote(
            glu16.at[pl.ds(rows - HALO, HALO)], halo_low, halo_send.at[0], halo_recv.at[0], ctx=c + 1
        )

    def halo_down():
        return remote(glu16.at[pl.ds(0, HALO)], halo_high, halo_send.at[1], halo_recv.at[1], ctx=c - 1)

    for step in range(ROW_CHUNKS):
        peer_copy(step).wait_recv()
        own = pl.ds(pl.multiple_of(c * rows + step * step_rows, 16), step_rows)
        summed = pair_sum[:, chunk(step), :].astype(jnp.float32) + peer_in[
            :, chunk(step), :
        ].astype(jnp.float32)
        middle[mine, chunk(step), :] = (
            gathered[mine, own, :].astype(jnp.float32) + summed
        ).astype(jnp.bfloat16)
        middle_copy(step, mine).start()
        middle_copy(step, others).wait_recv()

        def store(part, value):
            normed[chunk(step), part * cols : (part + 1) * cols] = value

        norm_rows(
            [middle[i, chunk(step), :].astype(jnp.float32) for i in range(tp_size)],
            conv_scale[...].reshape(1, -1),
            store,
        )
        halves = jnp.dot(normed[chunk(step), :], w_glu[...], preferred_element_type=jnp.float32)
        glu = (halves[:, :cols] * jax.nn.sigmoid(halves[:, cols:])).astype(jnp.bfloat16)
        glu16[chunk(step), :] = glu
        padded[HALO + step * step_rows : HALO + (step + 1) * step_rows, :] = glu.astype(jnp.float32)
        if step == 0:
            pl.when(has_down)(lambda: halo_down().start())
        if step == ROW_CHUNKS - 1:
            pl.when(has_up)(lambda: halo_up().start())

    def edge_low():
        padded[0:HALO, :] = jnp.zeros((HALO, cols), jnp.float32)

        @pl.when(has_down)
        def _():
            halo_up().wait_recv()
            padded[0:HALO, :] = halo_low[...].astype(jnp.float32)

    def edge_high():
        padded[HALO + rows :, :] = jnp.zeros((HALO, cols), jnp.float32)

        @pl.when(has_up)
        def _():
            halo_down().wait_recv()
            padded[HALO + rows :, :] = halo_high[...].astype(jnp.float32)

    def conv_pair(step):
        return stage(
            3, step, conv16.at[others, chunk(step)], conv_pair_in.at[:, chunk(step)], sibling
        )

    def conv_peer(step):
        return stage(4, step, conv_send.at[chunk(step)], conv_peer_in.at[chunk(step)], peer)

    tap_count = taps32.shape[0]
    first = HALO - tap_count // 2
    last_first = list(reversed(range(ROW_CHUNKS)))
    for step in last_first:
        if step == ROW_CHUNKS - 1:
            edge_high()
        if step == 0:
            edge_low()
        for lane in range(0, cols, 128):
            lanes = slice(lane, lane + 128)
            total = jnp.zeros((step_rows, 128), jnp.float32)
            for tap in range(tap_count):
                at = step * step_rows + first + tap
                total = total + padded[at : at + step_rows, lanes] * taps32[tap : tap + 1, lanes]
            total = total + bias[lanes].reshape(1, -1)
            act[chunk(step), lanes] = (total / (1.0 + jnp.exp(-total))).astype(jnp.bfloat16)
        terms = jnp.dot(act[chunk(step), :], w_proj[...], preferred_element_type=jnp.float32)
        for i in range(tp_size):
            piece = terms[:, i * cols : (i + 1) * cols]
            slot = (i % 2) * 2 + i // 2
            conv32[slot, chunk(step), :] = piece
            conv16[slot, chunk(step), :] = piece.astype(jnp.bfloat16)
        conv_pair(step).start()
    for step in last_first:
        conv_pair(step).wait_recv()
        conv_send[chunk(step), :] = (
            conv32[2 * k + 1 - y, chunk(step), :]
            + conv_pair_in[1 - y, chunk(step), :].astype(jnp.float32)
        ).astype(jnp.bfloat16)
        conv_peer(step).start()
        conv_keep[chunk(step), :] = (
            conv32[2 * k + y, chunk(step), :]
            + conv_pair_in[y, chunk(step), :].astype(jnp.float32)
            + middle[t, chunk(step), :].astype(jnp.float32)
        )
    for step in last_first:
        conv_peer(step).wait_recv()
        out[chunk(step), :] = (
            conv_keep[chunk(step), :] + conv_peer_in[chunk(step), :].astype(jnp.float32)
        ).astype(jnp.bfloat16)

    for place in range(ctx_size):
        index = pick(order, c, place)
        for part in range(PARTS):
            if place:
                along(index, part).wait_send()
            to_peer(index, part, block(index, t, part)).wait_send()
            to_sibling(index, y, part, block(index, t, part)).wait_send()
            to_sibling(index, 1 - y, part, block(index, t, part)).wait_send()
    for hop in range(1, ctx_size):
        for step in range(ROW_CHUNKS):
            context_copy((c + hop) % ctx_size, step).wait_send()
    for step in range(ROW_CHUNKS):
        pair_copy(step).wait_send()
        peer_copy(step).wait_send()
        middle_copy(step, mine).wait_send()
        conv_pair(step).wait_send()
        conv_peer(step).wait_send()
    pl.when(has_up)(lambda: halo_up().wait_send())
    pl.when(has_down)(lambda: halo_down().wait_send())


def fused(
    ctx_size,
    tp_size,
    frames,
    attn_gain,
    query_key_value,
    out_weight,
    conv_gain,
    glu_weight,
    depth_kernel,
    depth_bias,
    proj_weight,
):
    rows, cols = frames.shape
    width = cols * tp_size
    all_rows = rows * ctx_size
    taps = depth_kernel.shape[0]
    wide, narrow = jnp.float32, jnp.bfloat16
    vmem = pl.BlockSpec(memory_space=pltpu.VMEM)
    away = pl.BlockSpec(memory_space=pltpu.HBM)
    dma = pltpu.SemaphoreType.DMA
    return pl.pallas_call(
        functools.partial(fused_kernel, ctx_size, tp_size),
        out_shape=jax.ShapeDtypeStruct((rows, cols), narrow),
        in_specs=[away] * 9,
        out_specs=vmem,
        scratch_shapes=[
            pltpu.VMEM((width, 3 * WINDOW), narrow),
            pltpu.VMEM((width, 3 * SLOT), narrow),
            pltpu.VMEM((ctx_size * SLOT, width), narrow),
            pltpu.VMEM((width, 2 * cols), narrow),
            pltpu.VMEM((cols, width), narrow),
            pltpu.VMEM((taps, cols), narrow),
            pltpu.VMEM((taps, cols), wide),
            pltpu.VMEM((width,), wide),
            pltpu.VMEM((width,), wide),
            pltpu.VMEM((cols,), wide),
            pltpu.VMEM((tp_size, all_rows, cols), narrow),
            pltpu.VMEM((rows, width), narrow),
            pltpu.VMEM((ROW_CHUNKS, all_rows // ROW_CHUNKS, SLOT), narrow),
            pltpu.VMEM((all_rows, SLOT), narrow),
            pltpu.VMEM((SLOT, all_rows), narrow),
            pltpu.VMEM((all_rows, SLOT), narrow),
            pltpu.VMEM((all_rows // ROW_CHUNKS, all_rows), wide),
            pltpu.VMEM((ctx_size, rows, SLOT), narrow),
            pltpu.VMEM((rows, ctx_size * SLOT), narrow),
            pltpu.VMEM((tp_size, rows, cols), wide),
            pltpu.VMEM((tp_size, rows, cols), narrow),
            pltpu.VMEM((2, rows, cols), narrow),
            pltpu.VMEM((2, rows, cols), narrow),
            pltpu.VMEM((2, rows, cols), narrow),
            pltpu.VMEM((tp_size, rows, cols), narrow),
            pltpu.VMEM((rows, cols), narrow),
            pltpu.VMEM((HALO, cols), narrow),
            pltpu.VMEM((HALO, cols), narrow),
            pltpu.VMEM((rows + 2 * HALO, cols), wide),
            pltpu.VMEM((rows, cols), narrow),
            pltpu.VMEM((tp_size, rows, cols), wide),
            pltpu.VMEM((tp_size, rows, cols), narrow),
            pltpu.VMEM((2, rows, cols), narrow),
            pltpu.VMEM((rows, cols), wide),
            pltpu.VMEM((rows, cols), narrow),
            pltpu.VMEM((rows, cols), narrow),
            dma((12 + ctx_size,)),
            dma((ctx_size, tp_size, PARTS)),
            dma((ctx_size, 2, PARTS)),
            dma((ctx_size, PARTS)),
            dma((ctx_size, PARTS)),
            dma((ctx_size, ROW_CHUNKS)),
            dma((ctx_size, ROW_CHUNKS)),
            dma((5, ROW_CHUNKS)),
            dma((5, ROW_CHUNKS)),
            dma((2,)),
            dma((2,)),
        ],
        compiler_params=pltpu.CompilerParams(
            collective_id=0, has_side_effects=True, vmem_limit_bytes=62 * 1024 * 1024
        ),
    )(
        frames,
        attn_gain,
        query_key_value,
        out_weight,
        conv_gain,
        glu_weight,
        depth_kernel,
        depth_bias,
        proj_weight,
    )


def solution(mesh):
    in_specs = (
        P(("batch", "ctx"), "tp"),
        P(),
        P(None, None, "tp"),
        P("tp", None),
        P(),
        P(None, None, "tp"),
        P(None, "tp"),
        P("tp"),
        P("tp", None),
    )
    out_specs = P(("batch", "ctx"), "tp")
    ctx_size, tp_size = mesh.shape["ctx"], mesh.shape["tp"]

    def body(frames, attn_gain, query_key_value, *rest):
        one_head_each = ctx_size * HEAD == query_key_value.shape[2]
        even = frames.shape[0] % (16 * ROW_CHUNKS * PARTS) == 0
        if tp_size == 4 and one_head_each and ctx_size > 2 and even:
            return fused(ctx_size, tp_size, frames, attn_gain, query_key_value, *rest)
        return per_device(frames, attn_gain, query_key_value, *rest)

    return jax.shard_map(
        body, mesh=mesh, in_specs=in_specs, out_specs=out_specs, check_vma=False
    )
```
